256 devices in a mesh: chan: 32 (over z_lo, x, core), win: 8 (over y, z_hi).
Axes of the slice: x: 4, y: 4, z: 8 (z_hi: 2, z_lo: 4; z = z_hi * 4 + z_lo), core: 2. Of those that a mesh axis runs over, the one named last changes fastest.
Arguments:
- samples: bfloat16 [1024, 131072], P('chan', 'win'), may hold values from -6 to 6
- fir_taps: float32 [128], replicated, may hold values from -0.75 to 0.75
- tap_counts: int32 [8], P('win'), may hold values from 64 to 128, as said below
- band_start: int32 [1], replicated, may hold values from 1 to 7681
- grid_blocks: int32 [32], replicated, may hold values from 0 to 31, each once
Outputs:
- cross_spectra: bfloat16 [1024, 1024, 1024], P('chan', 'win')
The draws below stay inside these ranges and needn't reach their ends.
Inputs may be any that keep to these rules, and one draw needn't show every extreme that they name: `tap_counts`: at least one window uses all 128 taps. `grid_blocks`: each channel block is named once.
All inputs are finite; a program needn't handle non-finite values.
Results may differ from the reference program's by a relative error of at most 0.011.
Values may be sent and summed in bfloat16 or wider, within the bound.
No kernel may reach another device: no remote copies, remote signals or barrier semaphores. Data moves between devices by JAX's collectives and lax.ppermute only.
A program may use at most 64 MiB of HBM per device.

```python
import math
import jax
import jax.numpy as jnp
from jax import lax

CH_DEV = 32
LEN = 16384
FACTOR = 128
BAND = 512
KMAX = 128
CHANNELS = 1024
WINDOWS = 8
SAMPLES = 131072
N_CHAN = 32
N_WIN = 8


def draw_tap_counts(key, part):
    key = jax.random.fold_in(key, 7)
    span = KMAX - KMAX // 2 + 1
    order = jax.random.permutation(key, span).astype(jnp.int32)
    windows_index = jnp.arange(WINDOWS, dtype=jnp.int32)
    position = jnp.mod(windows_index, span)
    counts = KMAX // 2 + order[position]
    fullest = jax.random.randint(jax.random.fold_in(key, 11), (), 0, WINDOWS).astype(jnp.int32)
    return jnp.where(windows_index == fullest, KMAX, counts).astype(jnp.int32)


def block_scale(rng, extent, shards, low, largest):
    gain, own = 1.0, jax.random.fold_in(rng, 6)
    for dim, blocks in shards:
        heights = jnp.exp(jax.random.uniform(jax.random.fold_in(own, dim), (blocks,), jnp.float32, low / len(shards), largest / len(shards)))
        gain = gain * jnp.repeat(heights, extent[dim] // blocks).reshape([-1 if axis == dim else 1 for axis in range(len(extent))])
    return gain


def normal_values(rng, extent, scale, reach, shards=(), kind=jnp.bfloat16):
    entries = jax.random.normal(rng, extent, jnp.float32) * scale
    if len(shards) > 0:
        entries = block_scale(rng, extent, shards, -0.22, 0.18) * entries
    return jnp.clip(entries, min=-reach, max=reach).astype(kind)


def setup_inputs(seed: int = 0) -> dict:
    splits = jax.random.split(jax.random.key(seed), 6)
    return {
        "samples": normal_values(splits[0], (CHANNELS, SAMPLES), 1.0, 6.0, ((0, 32), (1, 8))),
        "fir_taps": normal_values(splits[1], (KMAX,), (KMAX // 2) ** -0.5, 0.75, (), jnp.float32),
        "tap_counts": draw_tap_counts(jax.random.fold_in(splits[5], 71), 0),
        "band_start": jax.random.randint(splits[3], (1,), 1, LEN // 2 - BAND + 2).astype(jnp.int32),
        "grid_blocks": jax.random.permutation(splits[4], N_CHAN).astype(jnp.int32),
    }


def fir_matrix(kept):
    lagged = jnp.arange(FACTOR, dtype=jnp.int32)[None, :] + FACTOR - jnp.arange(2 * FACTOR, dtype=jnp.int32)[:, None]
    taps_index = jnp.arange(KMAX, dtype=jnp.int32)
    picked = jnp.where(lagged[..., None] == taps_index, kept[..., None, None, :], 0.0)
    return lax.optimization_barrier(jnp.sum(picked, axis=-1)).astype(jnp.bfloat16)

def first_table():
    index = jnp.arange(FACTOR, dtype=jnp.int32)
    turns = jnp.mod(index[:, None] * index[None, :], FACTOR).astype(jnp.float32)
    angles = turns * (2.0 * math.pi / FACTOR)
    return jnp.stack([jnp.cos(angles), -jnp.sin(angles)]).astype(jnp.bfloat16)

def second_table(start):
    residue = jnp.arange(FACTOR, dtype=jnp.int32)[:, None]
    quarter = jnp.arange(BAND // FACTOR, dtype=jnp.int32)[None, :]
    freq = start + jnp.mod(residue - start, FACTOR) + FACTOR * quarter
    inner = jnp.arange(FACTOR, dtype=jnp.int32)
    turns = jnp.mod(freq[:, :, None] * inner[None, None, :], LEN).astype(jnp.float32)
    theta = turns * (2.0 * math.pi / LEN)
    cosine = jnp.cos(theta) / FACTOR
    sine = jnp.sin(theta) / FACTOR
    table = jnp.stack([jnp.stack([cosine, -sine]), jnp.stack([sine, cosine])])
    table = jnp.transpose(table, (2, 0, 4, 1, 3))
    return table.reshape(FACTOR, 2 * FACTOR, 2 * (BAND // FACTOR)).astype(jnp.bfloat16)

def whiten(product):
    width = BAND // FACTOR
    real_part = product[..., :width]
    imag_part = product[..., width:]
    scale = 1.0 / jnp.sqrt(real_part * real_part + imag_part * imag_part + 1.0)
    white = (product * jnp.concatenate([scale, scale], axis=-1)).astype(jnp.bfloat16)
    count = product.shape[1]
    white = white.reshape(FACTOR, count, 2, width)
    return jnp.transpose(white, (1, 2, 0, 3)).reshape(count, 2 * BAND)

def window_spectra(stacked, kept, start):
    matrix = fir_matrix(kept)
    filtered = jnp.einsum('caj,jb->cab', stacked.astype(jnp.float32), matrix.astype(jnp.float32)).astype(jnp.bfloat16)
    section = jnp.einsum('pra,cab->rcpb', first_table().astype(jnp.float32), filtered.astype(jnp.float32)).astype(jnp.bfloat16)
    section = section.reshape(FACTOR, section.shape[1], 2 * FACTOR)
    product = jnp.einsum('rcj,rjk->rck', section.astype(jnp.float32), second_table(start).astype(jnp.float32))
    return whiten(product)

def cross_block(left, right):
    left_re = left[..., :BAND]
    left_im = left[..., BAND:]
    right_re = right[..., :BAND]
    right_im = right[..., BAND:]
    real_part = jnp.einsum('wap,wbp->abp', left_re, right_re) + jnp.einsum('wap,wbp->abp', left_im, right_im)
    imag_part = jnp.einsum('wap,wbp->abp', left_im, right_re) - jnp.einsum('wap,wbp->abp', left_re, right_im)
    return jnp.concatenate([real_part, imag_part], axis=-1).astype(jnp.bfloat16)

def reference(samples, fir_taps, tap_counts, band_start, grid_blocks):
    count = samples.shape[0]
    segments = samples.reshape(count, N_WIN, LEN // FACTOR, FACTOR)
    window_tails = segments[:, :, -1, :]
    before = jnp.concatenate([jnp.zeros_like(window_tails[:, :1]), window_tails[:, :-1]], axis=1)
    previous = jnp.concatenate([before[:, :, None, :], segments[:, :, :-1, :]], axis=2)
    stacked = jnp.concatenate([previous, segments], axis=3)
    stacked = jnp.transpose(stacked, (1, 0, 2, 3))
    taps_index = jnp.arange(KMAX, dtype=jnp.int32)
    kept = fir_taps[None, :] * (taps_index[None, :] < tap_counts[:, None]).astype(jnp.float32)
    start = band_start[0]
    spectra = lax.map(lambda pair: window_spectra(pair[0], pair[1], start), (stacked, kept))
    ordered = jnp.take(spectra.reshape(N_WIN, N_CHAN, CH_DEV, 2 * BAND), grid_blocks, axis=1)
    ordered = ordered.reshape(N_WIN, count, 2 * BAND).astype(jnp.float32)

    def one_block(position):
        left = lax.dynamic_slice_in_dim(ordered, position * CH_DEV, CH_DEV, 1)
        return cross_block(left, ordered)
    blocks = lax.map(one_block, jnp.arange(N_CHAN, dtype=jnp.int32))
    return blocks.reshape(count, count, 2 * BAND)
```

```python
import functools
import math

import jax
import jax.numpy as jnp
import numpy as np
from jax import lax
from jax.experimental import pallas as pl
from jax.experimental.pallas import tpu as pltpu
from jax.sharding import PartitionSpec as P

LEN = 16384
FACTOR = 128
BAND = 512
KMAX = 128
COUNT = 32
QUARTERS = BAND // FACTOR
TURNS = QUARTERS + 1
WINDOWS = 8
LIMIT = 48 * 1024 * 1024

VMEM = pl.BlockSpec(memory_space=pltpu.VMEM)
SMEM = pl.BlockSpec(memory_space=pltpu.SMEM)
BF16 = jnp.bfloat16
F32 = jnp.float32


def tables():
    index = np.arange(FACTOR)
    turns = np.mod(index[:, None] * index[None, :], FACTOR)
    angles = turns * (2.0 * math.pi / FACTOR)
    cosine, sine = np.cos(angles), np.sin(angles)
    first = np.concatenate([cosine, -sine]).astype(BF16)
    theta = index[:, None] * index[None, :] * (2.0 * math.pi / LEN)
    twist = np.stack([np.cos(theta), -np.sin(theta)]).astype(np.float32)
    outer = np.stack([cosine, sine])[:, :72].astype(np.float32)
    place = np.arange(BAND)
    source = (place % QUARTERS) * FACTOR + place // QUARTERS
    interleave = np.zeros((BAND, BAND), np.float32)
    interleave[source, place] = 1.0
    return first, twist, outer, interleave.astype(BF16)


def dot(a, b):
    return jnp.dot(a, b, preferred_element_type=F32)


def dot_t(a, b):
    return lax.dot_general(a, b, (((1,), (1,)), ((), ())), preferred_element_type=F32)


def front_kernel(taps_used, start, taps, x, first, twist, outer, product, edge, head):
    lane = lax.broadcasted_iota(jnp.int32, (1, 2 * FACTOR), 1)
    kept = jnp.where(lane < taps_used[0], taps[...], 0.0)
    spread = jnp.broadcast_to(kept, (2 * FACTOR, 2 * FACTOR))
    matrix = pltpu.roll(spread, FACTOR, 1, stride=1, stride_axis=0)[:, :FACTOR].astype(BF16)
    head[...] = matrix[:FACTOR]
    both = jnp.concatenate([matrix[FACTOR:], matrix[:FACTOR]], axis=1)
    low = lax.shift_right_logical(start[0], 7)
    cosine = outer[0, pl.ds(low, 8), :]
    sine = outer[1, pl.ds(low, 8), :]
    scale = 1.0 / FACTOR
    second = jnp.concatenate(
        [jnp.concatenate([cosine, sine], axis=1), jnp.concatenate([-sine, cosine], axis=1)], axis=0
    )
    second = (second * scale).astype(BF16)
    twist_re = twist[0]
    twist_im = twist[1]
    for turn in range(TURNS):
        c = cosine[turn : turn + 1] * scale
        s = sine[turn : turn + 1] * scale
        edge[turn] = (twist_re * c + twist_im * s).astype(BF16)
        edge[TURNS + turn] = (twist_im * c - twist_re * s).astype(BF16)
    row = lax.broadcasted_iota(jnp.int32, (FACTOR, FACTOR), 0)

    def one(i, carry):
        parts = []
        for j in range(2):
            y = dot(x[2 * i + j], both)
            late = jnp.where(row == 0, 0.0, pltpu.roll(y[:, FACTOR:], 1, 0))
            parts.append((y[:, :FACTOR] + late).astype(BF16))
        section = dot(first[...], jnp.concatenate(parts, axis=1))
        halves = []
        for j in range(2):
            re = section[:FACTOR, j * FACTOR : (j + 1) * FACTOR]
            im = section[FACTOR:, j * FACTOR : (j + 1) * FACTOR]
            halves.append(
                jnp.concatenate([re * twist_re - im * twist_im, re * twist_im + im * twist_re], axis=1).astype(BF16)
            )
        got = dot_t(second, jnp.concatenate(halves, axis=0))
        for j in range(2):
            product[:, pl.ds(2 * i + j, 1), :] = got[:, None, j * FACTOR : (j + 1) * FACTOR]
        return carry

    lax.fori_loop(0, COUNT // 2, one, 0, unroll=2)


def whiten_kernel(start, product, edge, head, tail, interleave, out):
    extra = dot(tail[...], head[...]).astype(BF16)
    parts = []
    for o in range(2):
        for turn in range(TURNS):
            parts.append(product[8 * o + turn] + dot_t(extra, edge[TURNS * o + turn]))
    residue = lax.broadcasted_iota(jnp.int32, (COUNT, FACTOR), 1)
    early = residue >= (start[0] & (FACTOR - 1))
    white = [[], []]
    for q in range(QUARTERS):
        re = jnp.where(early, parts[q], parts[q + 1])
        im = jnp.where(early, parts[TURNS + q], parts[TURNS + q + 1])
        scale = lax.rsqrt(re * re + im * im + 1.0)
        white[0].append((re * scale).astype(BF16))
        white[1].append((im * scale).astype(BF16))
    flat = jnp.concatenate([jnp.concatenate(white[0], axis=1), jnp.concatenate(white[1], axis=1)], axis=0)
    placed = dot(flat, interleave[...])
    for z in range(4):
        for x in range(4):
            lanes = slice(x * FACTOR, (x + 1) * FACTOR)
            for core in range(2):
                at = (z * 2 + core) * 4
                piece = jnp.concatenate(
                    [placed[at : at + 4, lanes], placed[COUNT + at : COUNT + at + 4, lanes]], axis=0
                )
                out[z * 8 + x * 2 + core] = piece.astype(BF16)


def order_kernel(blocks, every, out):
    for i in range(COUNT):
        out[i] = every[blocks[i]]


M_STEP = 8


def cross_kernel(place, *refs):
    mine, theirs, rows = refs[:3]
    out, held, col, row = refs[-4:]
    step = pl.program_id(0)
    part = pl.program_id(1)
    chunk, z, core = place[0], place[1], place[2]

    @pl.when((step == 0) & (part == 0))
    def _():
        upper = lax.broadcasted_iota(jnp.int32, (8, FACTOR), 0) < 4
        first = core == 0

        def cols(w, carry):
            for other in range(4):
                d = z ^ other
                for b in range(4):
                    a = mine[d, w, b].astype(F32)
                    t = theirs[d, w, b].astype(F32)
                    c0 = jnp.where(first, a, t)
                    c1 = jnp.where(first, t, a)
                    col[w, 0, b * 4 + other] = jnp.where(upper, c0, pltpu.roll(c1, 4, 0))
                    col[w, 1, b * 4 + other] = jnp.where(upper, pltpu.roll(c0, 4, 0), c1)
            return carry

        lax.fori_loop(0, WINDOWS, cols, 0)

    @pl.when((part == 0))
    def _():
        upper = lax.broadcasted_iota(jnp.int32, (8, FACTOR), 0) < 4

        def rows_of(w, carry):
            at = step * 8 + chunk * 2
            c0 = rows[w, at].astype(F32)
            c1 = rows[w, at + 1].astype(F32)
            row[w, 0] = jnp.where(upper, c0, pltpu.roll(c1, 4, 0))
            row[w, 1] = jnp.where(upper, pltpu.roll(c0, 4, 0), c1)
            return carry

        lax.fori_loop(0, WINDOWS, rows_of, 0)

        def pair(t, carry):
            vr = [[col[w, 0, 2 * t + h] for w in range(WINDOWS)] for h in range(2)]
            vi = [[col[w, 1, 2 * t + h] for w in range(WINDOWS)] for h in range(2)]
            for m in range(M_STEP):
                re = [None, None]
                im = [None, None]
                for w in range(WINDOWS):
                    ur = row[w, 0, pl.ds(m, 1), :]
                    ui = row[w, 1, pl.ds(m, 1), :]
                    for h in range(2):
                        a = ur * vr[h][w] + ui * vi[h][w]
                        b = ui * vr[h][w] - ur * vi[h][w]
                        re[h] = a if w == 0 else re[h] + a
                        im[h] = b if w == 0 else im[h] + b
                out[m, pl.ds(pl.multiple_of(16 * t, 16), 16), :] = jnp.concatenate(re, axis=0).astype(BF16)
                held[m, pl.ds(pl.multiple_of(16 * t, 16), 16), :] = jnp.concatenate(im, axis=0).astype(BF16)
            return carry

        lax.fori_loop(0, 8, pair, 0)

    @pl.when(part == 1)
    def _():
        out[...] = held[...]


def cross(place, mine, theirs, rows, before):
    ins = [VMEM, VMEM, VMEM]
    args = [mine, theirs, rows]
    aliases = {}
    if before is not None:
        ins.append(pl.BlockSpec(memory_space=pl.ANY))
        args.append(before)
        aliases = {4: 0}
    return pl.pallas_call(
        cross_kernel,
        grid_spec=pltpu.PrefetchScalarGridSpec(
            num_scalar_prefetch=1,
            grid=(COUNT // M_STEP, 2),
            in_specs=ins,
            out_specs=pl.BlockSpec((M_STEP, 128, FACTOR), lambda s, o, place: (s, 0, place[0] + 4 * o)),
            scratch_shapes=[
                pltpu.VMEM((M_STEP, 128, FACTOR), BF16),
                pltpu.VMEM((WINDOWS, 2, 16, 8, FACTOR), F32),
                pltpu.VMEM((WINDOWS, 2, 8, FACTOR), F32),
            ],
        ),
        out_shape=jax.ShapeDtypeStruct((COUNT, 128, 2 * BAND), BF16),
        input_output_aliases=aliases,
        compiler_params=pltpu.CompilerParams(vmem_limit_bytes=LIMIT),
    )(place, *args)


def chan_swap(dz, dx, dc):
    spots = [(z, x, c) for z in range(4) for x in range(4) for c in range(2)]
    at = lambda z, x, c: z * 8 + x * 2 + c
    return [(at(z, x, c), at(z ^ dz, x ^ dx, c ^ dc)) for z, x, c in spots]


def shards(samples, fir_taps, tap_counts, band_start, grid_blocks):
    first, twist, outer, interleave = tables()
    tail = lax.ppermute(samples[:, -FACTOR:], "win", [(i, i + 1) for i in range(WINDOWS - 1)])
    product, edge, head = pl.pallas_call(
        front_kernel,
        in_specs=[SMEM, SMEM, VMEM, VMEM, VMEM, VMEM, VMEM],
        out_specs=[VMEM, VMEM, VMEM],
        out_shape=[
            jax.ShapeDtypeStruct((16, COUNT, FACTOR), F32),
            jax.ShapeDtypeStruct((2 * TURNS, FACTOR, FACTOR), BF16),
            jax.ShapeDtypeStruct((FACTOR, FACTOR), BF16),
        ],
        compiler_params=pltpu.CompilerParams(vmem_limit_bytes=LIMIT),
    )(
        tap_counts,
        band_start,
        jnp.pad(fir_taps, (0, FACTOR)).reshape(1, 2 * FACTOR),
        samples.reshape(COUNT, FACTOR, FACTOR),
        first,
        twist,
        outer,
    )
    pieces = pl.pallas_call(
        whiten_kernel,
        in_specs=[SMEM, VMEM, VMEM, VMEM, VMEM, VMEM],
        out_specs=VMEM,
        out_shape=jax.ShapeDtypeStruct((COUNT, 8, FACTOR), BF16),
        compiler_params=pltpu.CompilerParams(vmem_limit_bytes=LIMIT),
    )(band_start, product, edge, head, tail, interleave)
    every = lax.all_to_all(pieces, "chan", 0, 0, tiled=True)
    ordered = pl.pallas_call(
        order_kernel,
        in_specs=[SMEM, VMEM],
        out_specs=VMEM,
        out_shape=jax.ShapeDtypeStruct((COUNT, 8, FACTOR), BF16),
    )(grid_blocks, every)
    mine_rows = lax.all_to_all(ordered, "chan", 0, 0, tiled=True)
    sent = jnp.concatenate(
        [ordered.reshape(WINDOWS, 4, 8, FACTOR), jnp.broadcast_to(mine_rows[None], (WINDOWS, COUNT, 8, FACTOR))], axis=1
    )
    got = lax.all_to_all(sent, "win", 0, 0, tiled=True)
    cols, rows = got[:, :4], got[:, 4:]
    mine = [jnp.stack([cols] + [lax.ppermute(cols, "chan", chan_swap(d, 0, 0)) for d in (1, 2, 3)])]
    mine += [lax.ppermute(mine[0], "chan", chan_swap(0, d, 0)) for d in (1, 2, 3)]
    here = lax.axis_index("chan")
    z, x, core = here // 8, (here // 2) % 4, here % 2
    out = None
    for d in range(4):
        theirs = lax.ppermute(mine[d], "chan", chan_swap(0, 0, 1))
        place = jnp.stack([x ^ d, z, core]).astype(jnp.int32)
        out = cross(place, mine[d], theirs, rows, out)
    return out


def solution(mesh):
    placed = (P("chan", "win"), P(), P("win"), P(), P())
    return jax.shard_map(
        shards, mesh=mesh, in_specs=placed, out_specs=P("chan", "win", None), check_vma=False
    )
```

```python
import functools
import math

import jax
import jax.numpy as jnp
import numpy as np
from jax import lax
from jax.experimental import pallas as pl
from jax.experimental.pallas import tpu as pltpu
from jax.sharding import PartitionSpec as P

LEN = 16384
FACTOR = 128
BAND = 512
KMAX = 128
COUNT = 32
QUARTERS = BAND // FACTOR
TURNS = QUARTERS + 1
WINDOWS = 8
BATCH = 8
LIMIT = 48 * 1024 * 1024

VMEM = pl.BlockSpec(memory_space=pltpu.VMEM)
SMEM = pl.BlockSpec(memory_space=pltpu.SMEM)
HBM = pl.BlockSpec(memory_space=pltpu.HBM)
BF16 = jnp.bfloat16
F32 = jnp.float32


def tables():
    index = np.arange(FACTOR)
    turns = np.mod(index[:, None] * index[None, :], FACTOR)
    angles = turns * (2.0 * math.pi / FACTOR)
    cosine, sine = np.cos(angles), np.sin(angles)
    first = np.concatenate([cosine, -sine]).astype(BF16)
    theta = index[:, None] * index[None, :] * (2.0 * math.pi / LEN)
    twist = np.stack([np.cos(theta), -np.sin(theta)]).astype(np.float32)
    outer = np.stack([cosine, sine])[:, :72].astype(np.float32)
    place = np.arange(BAND)
    source = (place % QUARTERS) * FACTOR + place // QUARTERS
    interleave = np.zeros((BAND, BAND), np.float32)
    interleave[source, place] = 1.0
    return first, twist, outer, interleave.astype(BF16)


def dot(a, b):
    return jnp.dot(a, b, preferred_element_type=F32)


def dot_t(a, b):
    return lax.dot_general(a, b, (((1,), (1,)), ((), ())), preferred_element_type=F32)


def front_kernel(
    used_in, start_in, taps_in, x, first_in, twist_in, outer_in,
    product, edge, head, taps_used, start, taps, first, twist, outer, sems,
):
    copies = [
        pltpu.make_async_copy(source, target, sems.at[i])
        for i, (source, target) in enumerate(
            (
                (used_in, taps_used),
                (start_in, start),
                (taps_in, taps),
                (outer_in, outer),
                (twist_in, twist),
                (first_in, first),
            )
        )
    ]
    for copy in copies:
        copy.start()
    for copy in copies[:3]:
        copy.wait()
    lane = lax.broadcasted_iota(jnp.int32, (1, FACTOR), 1)
    kept = jnp.where(lane < taps_used[0], taps[...], 0.0)
    kept = jnp.concatenate([kept, jnp.zeros_like(kept)], axis=1)
    spread = jnp.broadcast_to(kept, (2 * FACTOR, 2 * FACTOR))
    matrix = pltpu.roll(spread, FACTOR, 1, stride=1, stride_axis=0)[:, :FACTOR].astype(BF16)
    head[...] = matrix[:FACTOR]
    both = jnp.concatenate([matrix[FACTOR:], matrix[:FACTOR]], axis=1)
    low = lax.shift_right_logical(start[0], 7)
    for copy in copies[3:]:
        copy.wait()
    cosine = outer[0, pl.ds(low, 8), :]
    sine = outer[1, pl.ds(low, 8), :]
    scale = 1.0 / FACTOR
    second = jnp.concatenate(
        [jnp.concatenate([cosine, sine], axis=1), jnp.concatenate([-sine, cosine], axis=1)], axis=0
    )
    second = (second * scale).astype(BF16)
    twist_re = twist[0]
    twist_im = twist[1]
    for turn in range(TURNS):
        c = cosine[turn : turn + 1] * scale
        s = sine[turn : turn + 1] * scale
        edge[turn] = (twist_re * c + twist_im * s).astype(BF16)
        edge[TURNS + turn] = (twist_im * c - twist_re * s).astype(BF16)
    row = lax.broadcasted_iota(jnp.int32, (FACTOR, FACTOR), 0)

    def some(i, carry):
        y = dot(x[pl.ds(BATCH * i, BATCH)].reshape(BATCH * FACTOR, FACTOR), both)
        parts = []
        for j in range(BATCH):
            now = y[j * FACTOR : (j + 1) * FACTOR]
            late = jnp.where(row == 0, 0.0, pltpu.roll(now[:, FACTOR:], 1, 0))
            parts.append((now[:, :FACTOR] + late).astype(BF16))
        section = dot(first[...], jnp.concatenate(parts, axis=1))
        halves = []
        for j in range(BATCH):
            re = section[:FACTOR, j * FACTOR : (j + 1) * FACTOR]
            im = section[FACTOR:, j * FACTOR : (j + 1) * FACTOR]
            halves.append(
                jnp.concatenate([re * twist_re - im * twist_im, re * twist_im + im * twist_re], axis=1).astype(BF16)
            )
        got = dot_t(second, jnp.concatenate(halves, axis=0))
        for j in range(BATCH):
            product[:, pl.ds(BATCH * i + j, 1), :] = got[:, None, j * FACTOR : (j + 1) * FACTOR]
        return carry

    lax.fori_loop(0, COUNT // BATCH, some, 0)


def whiten_kernel(start_in, blocks_in, product, edge, head, tail, interleave_in, out, blocks, interleave, start, sems):
    copies = [
        pltpu.make_async_copy(source, target, sems.at[i])
        for i, (source, target) in enumerate(((start_in, start), (blocks_in, blocks), (interleave_in, interleave)))
    ]
    for copy in copies:
        copy.start()
    extra = dot(tail[...], head[...]).astype(BF16)
    parts = []
    for o in range(2):
        for turn in range(TURNS):
            parts.append(product[8 * o + turn] + dot_t(extra, edge[TURNS * o + turn]))
    for copy in copies:
        copy.wait()
    residue = lax.broadcasted_iota(jnp.int32, (COUNT, FACTOR), 1)
    early = residue >= (start[0] & (FACTOR - 1))
    white = [[], []]
    for q in range(QUARTERS):
        re = jnp.where(early, parts[q], parts[q + 1])
        im = jnp.where(early, parts[TURNS + q], parts[TURNS + q + 1])
        scale = lax.rsqrt(re * re + im * im + 1.0)
        white[0].append((re * scale).astype(BF16))
        white[1].append((im * scale).astype(BF16))
    flat = jnp.concatenate([jnp.concatenate(white[0], axis=1), jnp.concatenate(white[1], axis=1)], axis=0)
    placed = dot(flat, interleave[...])
    for z in range(4):
        for x in range(4):
            lanes = slice(x * FACTOR, (x + 1) * FACTOR)
            for core in range(2):
                at = (z * 2 + core) * 4
                piece = jnp.concatenate(
                    [placed[at : at + 4, lanes], placed[COUNT + at : COUNT + at + 4, lanes]], axis=0
                )
                out[z * 8 + x * 2 + core] = piece.astype(BF16)


def order_kernel(blocks, every, out):
    for i in range(COUNT):
        out[i] = every[blocks[i]]


M_STEP = 8
GROUPS = 8
WIDTH = FACTOR // GROUPS


def spiral(parts, bits):
    for s in range(3):
        parts = [jnp.where(bits[s], parts[(a + (1 << s)) % GROUPS], parts[a]) for a in range(GROUPS)]
    return parts


def cross_kernel(parts, place, *refs):
    count = len(parts)
    mine, theirs, rows = refs[:count], refs[count : 2 * count], refs[2 * count]
    out, left, coef, mixed, stage, done = refs[-6:]
    x, z, core = place[0], place[1], place[2]
    upper = lax.broadcasted_iota(jnp.int32, (8, FACTOR), 0) < 4
    spot = lax.broadcasted_iota(jnp.int32, (8, FACTOR), 1) // WIDTH
    bits = [(spot & (1 << s)) != 0 for s in range(3)]
    inner = lax.broadcasted_iota(jnp.int32, (WIDTH, FACTOR), 0)
    lane = lax.broadcasted_iota(jnp.int32, (WIDTH, FACTOR), 1)
    diagonal = inner == (lane & (WIDTH - 1))

    def join(c0, c1):
        return jnp.where(upper, c0, pltpu.roll(c1, 4, 0)), jnp.where(upper, pltpu.roll(c0, 4, 0), c1)

    def cols(part, b, carry):
        for pair in range(2):
            tiles = []
            for half in range(2):
                d = z ^ (2 * pair + half)
                whole = [[], []]
                for w in range(WINDOWS):
                    a = mine[part][d, w, b].astype(F32)
                    t = theirs[part][d, w, b].astype(F32)
                    re, im = join(jnp.where(core == 0, a, t), jnp.where(core == 0, t, a))
                    whole[0].append(pltpu.roll(re, WIDTH * w, 1) if w else re)
                    whole[1].append(pltpu.roll(im, WIDTH * w, 1) if w else im)
                tiles.append([spiral(whole[i], bits) for i in range(2)])
            at = pl.multiple_of(b * 32 + pair * 16, 16)
            for g in range(GROUPS):
                for i in range(2):
                    packed = jnp.concatenate([tiles[h][i][-g % GROUPS] for h in range(2)], axis=0)
                    left[part, g, pl.ds(at, 16), i * FACTOR : (i + 1) * FACTOR] = packed.astype(BF16)
        return carry

    for part in range(count):
        lax.fori_loop(0, 4, functools.partial(cols, part), 0)

    def chunk_of(part):
        turn = jnp.int32(parts[0])
        for i in range(1, count):
            turn = jnp.where(part == i, parts[i], turn)
        return x ^ turn

    def multiply(step, slot):
        part = lax.shift_right_logical(step, 2)
        at = (step & 3) * 8 + chunk_of(part) * 2
        for w in range(WINDOWS):
            re, im = join(rows[w, at].astype(F32), rows[w, at + 1].astype(F32))
            for i, u in enumerate((re, im)):
                u = pltpu.roll(u, 0, 1, stride=WIDTH, stride_axis=0)
                for s in range(3):
                    u = jnp.where(bits[s], pltpu.roll(u, 8 - (1 << s), 0), u)
                coef[slot, w, i] = u
                if i == 0:
                    coef[slot, w, 2] = -u
        for g in range(GROUPS):
            blocks = [
                [
                    jnp.where(diagonal, coef[slot, w, i, pl.ds(-g % GROUPS, 1), :], 0.0).astype(BF16)
                    for i in range(3)
                ]
                for w in range(WINDOWS)
            ]
            order = [blocks[(c - g) % GROUPS] for c in range(GROUPS)]
            top = jnp.concatenate([jnp.concatenate([k[0], k[1]], axis=1) for k in order], axis=0)
            low = jnp.concatenate([jnp.concatenate([k[1], k[2]], axis=1) for k in order], axis=0)
            mixed[slot, g] = dot(left[part, g], jnp.concatenate([top, low], axis=0))

    def copies(step, slot):
        chunk = chunk_of(lax.shift_right_logical(step, 2))
        for o in range(2):
            lanes = pl.ds(pl.multiple_of((chunk + 4 * o) * FACTOR, FACTOR), FACTOR)
            yield pltpu.make_async_copy(
                stage.at[slot, o], out.at[pl.ds((step & 3) * M_STEP, M_STEP), :, lanes], done.at[slot, o]
            )

    def spread(slot):
        for t in range(8):
            for o in range(2):
                halves = []
                for h in range(2):
                    lanes = slice(o * FACTOR, (o + 1) * FACTOR)
                    parts = [mixed[slot, g, 16 * t + 8 * h : 16 * t + 8 * h + 8, lanes] for g in range(GROUPS)]
                    halves.append(spiral(parts, bits))
                for m in range(M_STEP):
                    pair = [pltpu.roll(x[-m % GROUPS], FACTOR - WIDTH * m, 1) if m else x[0] for x in halves]
                    stage[slot, o, m, 16 * t : 16 * t + 16, :] = jnp.concatenate(pair, axis=0).astype(BF16)

    steps = count * (COUNT // M_STEP)
    multiply(jnp.int32(0), 0)

    def both(i, carry):
        for slot in range(2):
            step = 2 * i + slot

            @pl.when(i > 0)
            def _():
                for copy in copies(step - 2, slot):
                    copy.wait()

            multiply(jnp.minimum(step + 1, steps - 1), 1 - slot)
            spread(slot)
            for copy in copies(step, slot):
                copy.start()
        return carry

    lax.fori_loop(0, steps // 2, both, 0)
    for slot in range(2):
        for copy in copies(jnp.int32(steps - 2 + slot), slot):
            copy.wait()


def cross(parts, place, mine, theirs, rows, before):
    args = [place, *mine, *theirs, rows]
    specs = [SMEM] + [VMEM] * (len(args) - 1)
    aliases = {}
    if before is not None:
        aliases = {len(args): 0}
        args.append(before)
        specs.append(pl.BlockSpec(memory_space=pl.ANY))
    return pl.pallas_call(
        functools.partial(cross_kernel, parts),
        in_specs=specs,
        out_specs=pl.BlockSpec(memory_space=pl.ANY),
        scratch_shapes=[
            pltpu.VMEM((len(parts), GROUPS, FACTOR, 2 * FACTOR), BF16),
            pltpu.VMEM((2, WINDOWS, 3, 8, FACTOR), F32),
            pltpu.VMEM((2, GROUPS, FACTOR, 2 * FACTOR), F32),
            pltpu.VMEM((2, 2, M_STEP, FACTOR, FACTOR), BF16),
            pltpu.SemaphoreType.DMA((2, 2)),
        ],
        out_shape=jax.ShapeDtypeStruct((COUNT, 128, 2 * BAND), BF16),
        input_output_aliases=aliases,
        compiler_params=pltpu.CompilerParams(vmem_limit_bytes=LIMIT),
    )(*args)


def chan_swap(dz, dx, dc):
    spots = [(z, x, c) for z in range(4) for x in range(4) for c in range(2)]
    at = lambda z, x, c: z * 8 + x * 2 + c
    return [(at(z, x, c), at(z ^ dz, x ^ dx, c ^ dc)) for z, x, c in spots]


def shards(samples, fir_taps, tap_counts, band_start, grid_blocks):
    first, twist, outer, interleave = tables()
    tail = lax.ppermute(samples[:, -FACTOR:], "win", [(i, i + 1) for i in range(WINDOWS - 1)])
    product, edge, head = pl.pallas_call(
        front_kernel,
        in_specs=[HBM, HBM, HBM, VMEM, HBM, HBM, HBM],
        out_specs=[VMEM, VMEM, VMEM],
        out_shape=[
            jax.ShapeDtypeStruct((16, COUNT, FACTOR), F32),
            jax.ShapeDtypeStruct((2 * TURNS, FACTOR, FACTOR), BF16),
            jax.ShapeDtypeStruct((FACTOR, FACTOR), BF16),
        ],
        scratch_shapes=[
            pltpu.SMEM((1,), jnp.int32),
            pltpu.SMEM((1,), jnp.int32),
            pltpu.VMEM((1, FACTOR), F32),
            pltpu.VMEM(first.shape, BF16),
            pltpu.VMEM(twist.shape, F32),
            pltpu.VMEM(outer.shape, F32),
            pltpu.SemaphoreType.DMA((6,)),
        ],
        compiler_params=pltpu.CompilerParams(vmem_limit_bytes=LIMIT),
    )(
        tap_counts,
        band_start,
        fir_taps.reshape(1, FACTOR),
        samples.reshape(COUNT, FACTOR, FACTOR),
        first,
        twist,
        outer,
    )
    pieces, blocks = pl.pallas_call(
        whiten_kernel,
        in_specs=[HBM, HBM, VMEM, VMEM, VMEM, VMEM, HBM],
        scratch_shapes=[
            pltpu.VMEM((BAND, BAND), BF16),
            pltpu.SMEM((1,), jnp.int32),
            pltpu.SemaphoreType.DMA((3,)),
        ],
        out_specs=[VMEM, SMEM],
        out_shape=[
            jax.ShapeDtypeStruct((COUNT, 8, FACTOR), BF16),
            jax.ShapeDtypeStruct((COUNT,), jnp.int32),
        ],
        compiler_params=pltpu.CompilerParams(vmem_limit_bytes=LIMIT),
    )(band_start, grid_blocks, product, edge, head, tail, interleave)
    every = lax.all_to_all(pieces, "chan", 0, 0, tiled=True)
    ordered = pl.pallas_call(
        order_kernel,
        in_specs=[SMEM, VMEM],
        out_specs=VMEM,
        out_shape=jax.ShapeDtypeStruct((COUNT, 8, FACTOR), BF16),
    )(blocks, every)
    cols = lax.all_to_all(ordered.reshape(WINDOWS, 4, 8, FACTOR), "win", 0, 0, tiled=True)
    ordered, cols = lax.optimization_barrier((ordered, cols))
    near = [lax.ppermute(cols, "chan", chan_swap(d, 0, 0)) for d in (1, 2, 3)]
    rows = lax.all_to_all(ordered, "chan", 0, 0, tiled=True)
    rows, near = lax.optimization_barrier((rows, near))
    mine = [jnp.stack([cols] + near)]
    mine += [lax.ppermute(mine[0], "chan", chan_swap(0, d, 0)) for d in (1, 2, 3)]
    theirs = [lax.ppermute(this, "chan", chan_swap(0, 0, 1)) for this in mine]
    rows = lax.all_to_all(
        jnp.broadcast_to(rows[None], (WINDOWS, COUNT, 8, FACTOR)), "win", 0, 0, tiled=True
    )
    here = lax.axis_index("chan")
    place = jnp.stack([(here // 2) % 4, here // 8, here % 2]).astype(jnp.int32)
    return cross((0, 1, 2, 3), place, mine, theirs, rows, None)


def solution(mesh):
    placed = (P("chan", "win"), P(), P("win"), P(), P())
    return jax.shard_map(
        shards, mesh=mesh, in_specs=placed, out_specs=P("chan", "win", None), check_vma=False
    )
```

```python
import functools
import math

import jax
import jax.numpy as jnp
import numpy as np
from jax import lax
from jax.experimental import pallas as pl
from jax.experimental.pallas import tpu as pltpu
from jax.sharding import PartitionSpec as P

LEN = 16384
FACTOR = 128
BAND = 512
KMAX = 128
COUNT = 32
QUARTERS = BAND // FACTOR
WINDOWS = 8
BATCH = 8
GROUPS = 8
WIDTH = FACTOR // GROUPS
SLOTS = 4
LIMIT = 48 * 1024 * 1024

VMEM = pl.BlockSpec(memory_space=pltpu.VMEM)
SMEM = pl.BlockSpec(memory_space=pltpu.SMEM)
BF16 = jnp.bfloat16
F32 = jnp.float32


def tables():
    index = np.arange(FACTOR)
    angles = np.mod(index[:, None] * index[None, :], FACTOR) * (2.0 * math.pi / FACTOR)
    theta = index[:, None] * index[None, :] * (2.0 * math.pi / LEN)
    parts = [np.cos(angles), -np.sin(angles), np.cos(theta), -np.sin(theta)]
    return np.concatenate(parts).astype(np.float32)


def dot(a, b):
    return jnp.dot(a, b, preferred_element_type=F32)


def dot_t(a, b):
    return lax.dot_general(a, b, (((1,), (1,)), ((), ())), preferred_element_type=F32)


def front_kernel(taps_used, start, window, taps, x, tail, table, out, product, before):
    lane = lax.broadcasted_iota(jnp.int32, (1, FACTOR), 1)
    kept = jnp.where(lane < taps_used[0], taps[...], 0.0)
    kept = jnp.concatenate([kept, jnp.zeros_like(kept)], axis=1)
    spread = jnp.broadcast_to(kept, (2 * FACTOR, 2 * FACTOR))
    matrix = pltpu.roll(spread, FACTOR, 1, stride=1, stride_axis=0)[:, :FACTOR].astype(BF16)
    both = jnp.concatenate([matrix[FACTOR:], matrix[:FACTOR]], axis=1)
    before[...] = dot(tail[...], matrix[:FACTOR])
    first = table[: 2 * FACTOR].astype(BF16)
    low = lax.shift_right_logical(start[0], 7)
    row = lax.broadcasted_iota(jnp.int32, (8, FACTOR), 0)
    pick = (lax.broadcasted_iota(jnp.int32, (8, FACTOR), 1) == low + row).astype(F32).astype(BF16)
    cosine = dot(pick, first[:FACTOR])
    sine = dot(pick, first[FACTOR:])
    second = jnp.concatenate(
        [jnp.concatenate([cosine, -sine], axis=1), jnp.concatenate([sine, cosine], axis=1)], axis=0
    )
    second = (second * (1.0 / FACTOR)).astype(BF16)
    top = lax.broadcasted_iota(jnp.int32, (FACTOR, FACTOR), 0) == 0

    def some(i, carry):
        y = dot(x[pl.ds(BATCH * i, BATCH)].reshape(BATCH * FACTOR, FACTOR), both)
        parts = []
        for j in range(BATCH):
            now = y[j * FACTOR : (j + 1) * FACTOR]
            late = jnp.where(top, before[pl.ds(BATCH * i + j, 1), :], pltpu.roll(now[:, FACTOR:], 1, 0))
            parts.append((now[:, :FACTOR] + late).astype(BF16))
        section = dot(first, jnp.concatenate(parts, axis=1))
        halves = []
        for j in range(BATCH):
            re = section[:FACTOR, j * FACTOR : (j + 1) * FACTOR]
            im = section[FACTOR:, j * FACTOR : (j + 1) * FACTOR]
            twist_re = table[2 * FACTOR : 3 * FACTOR]
            twist_im = table[3 * FACTOR :]
            halves.append(
                jnp.concatenate([re * twist_re - im * twist_im, re * twist_im + im * twist_re], axis=1).astype(BF16)
            )
        got = dot_t(second, jnp.concatenate(halves, axis=0))
        for j in range(BATCH):
            product[:, pl.ds(BATCH * i + j, 1), :] = got[:, None, j * FACTOR : (j + 1) * FACTOR]
        return carry

    lax.fori_loop(0, COUNT // BATCH, some, 0)

    early = lax.broadcasted_iota(jnp.int32, (COUNT, FACTOR), 1) >= (start[0] & (FACTOR - 1))
    residue = lax.broadcasted_iota(jnp.int32, (FACTOR, BAND), 0)
    lane = lax.broadcasted_iota(jnp.int32, (FACTOR, BAND), 1)
    place = (lane & -FACTOR) + ((lane - WIDTH * window[0]) & (FACTOR - 1))
    placed = None
    for q in range(QUARTERS):
        re = jnp.where(early, product[q], product[q + 1])
        im = jnp.where(early, product[8 + q], product[9 + q])
        scale = lax.rsqrt(re * re + im * im + 1.0)
        white = jnp.concatenate([re * scale, im * scale], axis=0).astype(BF16)
        moved = dot(white, (place == QUARTERS * residue + q).astype(F32).astype(BF16))
        placed = moved if placed is None else placed + moved
    for z in range(4):
        for quarter in range(4):
            for o in range(2):
                at = o * COUNT + z * 8
                piece = placed[at : at + 8, quarter * FACTOR : (quarter + 1) * FACTOR]
                out[z * 8 + quarter * 2 + o] = piece.astype(BF16)


def order_kernel(blocks, every, out):
    for i in range(COUNT):
        out[i] = every[blocks[i]]


M_STEP = 8


def spiral(parts, bits):
    for s in range(3):
        parts = [jnp.where(bits[s], parts[(a + (1 << s)) % GROUPS], parts[a]) for a in range(GROUPS)]
    return parts


def cross_kernel(parts, place, *refs):
    count = len(parts)
    mine, theirs, rows = refs[:count], refs[count : 2 * count], refs[2 * count]
    out, left, coef, mixed, stage, done = refs[-6:]
    x, z, core = place[0], place[1], place[2]
    spot = lax.broadcasted_iota(jnp.int32, (8, FACTOR), 1) // WIDTH
    bits = [(spot & (1 << s)) != 0 for s in range(3)]
    inner = lax.broadcasted_iota(jnp.int32, (WIDTH, FACTOR), 0)
    lane = lax.broadcasted_iota(jnp.int32, (WIDTH, FACTOR), 1)
    diagonal = inner == (lane & (WIDTH - 1))

    def cols(part, b, carry):
        for pair in range(2):
            tiles = []
            for half in range(2):
                d = z ^ (2 * pair + half)
                whole = [[], []]
                for w in range(WINDOWS):
                    a = mine[part][d, w, b].astype(F32)
                    t = theirs[part][d, w, b].astype(F32)
                    whole[0].append(jnp.where(core == 0, a, t))
                    whole[1].append(jnp.where(core == 0, t, a))
                tiles.append([spiral(whole[i], bits) for i in range(2)])
            at = pl.multiple_of(b * 32 + pair * 16, 16)
            for g in range(GROUPS):
                for i in range(2):
                    packed = jnp.concatenate([tiles[h][i][-g % GROUPS] for h in range(2)], axis=0)
                    left[part, g, pl.ds(at, 16), i * FACTOR : (i + 1) * FACTOR] = packed.astype(BF16)
        return carry

    for part in range(count):
        lax.fori_loop(0, 4, functools.partial(cols, part), 0)

    def chunk_of(part):
        turn = jnp.int32(parts[0])
        for i in range(1, count):
            turn = jnp.where(part == i, parts[i], turn)
        return x ^ turn

    def multiply(step, slot):
        part = lax.shift_right_logical(step, 2)
        at = (step & 3) * 8 + chunk_of(part) * 2
        for w in range(WINDOWS):
            for i in range(2):
                u = rows[w, at + i].astype(F32)
                if w:
                    u = pltpu.roll(u, FACTOR - WIDTH * w, 1)
                u = pltpu.roll(u, 0, 1, stride=WIDTH, stride_axis=0)
                for s in range(3):
                    u = jnp.where(bits[s], pltpu.roll(u, 8 - (1 << s), 0), u)
                coef[slot, w, i] = u
                if i == 0:
                    coef[slot, w, 2] = -u
        for g in range(GROUPS):
            blocks = [
                [
                    jnp.where(diagonal, coef[slot, w, i, pl.ds(-g % GROUPS, 1), :], 0.0).astype(BF16)
                    for i in range(3)
                ]
                for w in range(WINDOWS)
            ]
            order = [blocks[(c - g) % GROUPS] for c in range(GROUPS)]
            top = jnp.concatenate([jnp.concatenate([k[0], k[1]], axis=1) for k in order], axis=0)
            low = jnp.concatenate([jnp.concatenate([k[1], k[2]], axis=1) for k in order], axis=0)
            mixed[slot, g] = dot(left[part, g], jnp.concatenate([top, low], axis=0))

    def copies(step):
        slot = step % SLOTS
        chunk = chunk_of(lax.shift_right_logical(step, 2))
        for o in range(2):
            lanes = pl.ds(pl.multiple_of((chunk + 4 * o) * FACTOR, FACTOR), FACTOR)
            yield pltpu.make_async_copy(
                stage.at[slot, o], out.at[pl.ds((step & 3) * M_STEP, M_STEP), :, lanes], done.at[slot, o]
            )

    def spread(slot, step):
        target = step % SLOTS
        for t in range(8):
            for o in range(2):
                halves = []
                for h in range(2):
                    lanes = slice(o * FACTOR, (o + 1) * FACTOR)
                    parts = [mixed[slot, g, 16 * t + 8 * h : 16 * t + 8 * h + 8, lanes] for g in range(GROUPS)]
                    halves.append(spiral(parts, bits))
                for m in range(M_STEP):
                    pair = [pltpu.roll(x[-m % GROUPS], FACTOR - WIDTH * m, 1) if m else x[0] for x in halves]
                    stage[target, o, m, 16 * t : 16 * t + 16, :] = jnp.concatenate(pair, axis=0).astype(BF16)

    steps = count * (COUNT // M_STEP)
    multiply(jnp.int32(0), 0)

    def both(i, carry):
        for slot in range(2):
            step = 2 * i + slot

            @pl.when(step >= SLOTS)
            def _():
                for copy in copies(step - SLOTS):
                    copy.wait()

            multiply(jnp.minimum(step + 1, steps - 1), 1 - slot)
            spread(slot, step)
            for copy in copies(step):
                copy.start()
        return carry

    lax.fori_loop(0, steps // 2, both, 0)
    for step in range(steps - SLOTS, steps):
        for copy in copies(jnp.int32(step)):
            copy.wait()


def cross(parts, place, mine, theirs, rows, before):
    args = [place, *mine, *theirs, rows]
    specs = [SMEM] + [VMEM] * (len(args) - 1)
    aliases = {}
    if before is not None:
        aliases = {len(args): 0}
        args.append(before)
        specs.append(pl.BlockSpec(memory_space=pl.ANY))
    return pl.pallas_call(
        functools.partial(cross_kernel, parts),
        in_specs=specs,
        out_specs=pl.BlockSpec(memory_space=pl.ANY),
        scratch_shapes=[
            pltpu.VMEM((len(parts), GROUPS, FACTOR, 2 * FACTOR), BF16),
            pltpu.VMEM((2, WINDOWS, 3, 8, FACTOR), F32),
            pltpu.VMEM((2, GROUPS, FACTOR, 2 * FACTOR), F32),
            pltpu.VMEM((SLOTS, 2, M_STEP, FACTOR, FACTOR), BF16),
            pltpu.SemaphoreType.DMA((SLOTS, 2)),
        ],
        out_shape=jax.ShapeDtypeStruct((COUNT, 128, 2 * BAND), BF16),
        input_output_aliases=aliases,
        compiler_params=pltpu.CompilerParams(vmem_limit_bytes=LIMIT),
    )(*args)


def chan_swap(dz, dx, dc):
    spots = [(z, x, c) for z in range(4) for x in range(4) for c in range(2)]
    at = lambda z, x, c: z * 8 + x * 2 + c
    return [(at(z, x, c), at(z ^ dz, x ^ dx, c ^ dc)) for z, x, c in spots]


def shards(samples, fir_taps, tap_counts, band_start, grid_blocks):
    tail = lax.ppermute(samples[:, -FACTOR:], "win", [(i, i + 1) for i in range(WINDOWS - 1)])
    pieces = pl.pallas_call(
        front_kernel,
        in_specs=[SMEM, SMEM, SMEM, VMEM, VMEM, VMEM, VMEM],
        out_specs=VMEM,
        out_shape=jax.ShapeDtypeStruct((COUNT, 8, FACTOR), BF16),
        scratch_shapes=[pltpu.VMEM((16, COUNT, FACTOR), F32), pltpu.VMEM((COUNT, FACTOR), F32)],
        compiler_params=pltpu.CompilerParams(vmem_limit_bytes=LIMIT),
    )(
        tap_counts,
        band_start,
        lax.axis_index("win").reshape(1),
        fir_taps.reshape(1, FACTOR),
        samples.reshape(COUNT, FACTOR, FACTOR),
        tail,
        tables(),
    )
    every = lax.all_to_all(pieces, "chan", 0, 0, tiled=True)
    ordered = pl.pallas_call(
        order_kernel,
        in_specs=[SMEM, VMEM],
        out_specs=VMEM,
        out_shape=jax.ShapeDtypeStruct((COUNT, 8, FACTOR), BF16),
    )(grid_blocks, every)
    cols = lax.all_to_all(ordered.reshape(WINDOWS, 4, 8, FACTOR), "win", 0, 0, tiled=True)
    ordered, cols = lax.optimization_barrier((ordered, cols))
    near = [lax.ppermute(cols, "chan", chan_swap(d, 0, 0)) for d in (1, 2, 3)]
    rows = lax.all_to_all(ordered, "chan", 0, 0, tiled=True)
    rows, near = lax.optimization_barrier((rows, near))
    mine = [jnp.stack([cols] + near)]
    mine += [lax.ppermute(mine[0], "chan", chan_swap(0, d, 0)) for d in (1, 2, 3)]
    theirs = [lax.ppermute(this, "chan", chan_swap(0, 0, 1)) for this in mine]
    rows = lax.all_to_all(
        jnp.broadcast_to(rows[None], (WINDOWS, COUNT, 8, FACTOR)), "win", 0, 0, tiled=True
    )
    here = lax.axis_index("chan")
    place = jnp.stack([(here // 2) % 4, here // 8, here % 2]).astype(jnp.int32)
    return cross((0, 1, 2, 3), place, mine, theirs, rows, None)


def solution(mesh):
    placed = (P("chan", "win"), P(), P("win"), P(), P())
    return jax.shard_map(
        shards, mesh=mesh, in_specs=placed, out_specs=P("chan", "win", None), check_vma=False
    )
```

```python
import functools
import math

import jax
import jax.numpy as jnp
import numpy as np
from jax import lax
from jax.experimental import pallas as pl
from jax.experimental.pallas import tpu as pltpu
from jax.sharding import PartitionSpec as P

LEN = 16384
FACTOR = 128
BAND = 512
KMAX = 128
COUNT = 32
QUARTERS = BAND // FACTOR
WINDOWS = 8
BATCH = 8
GROUPS = 8
WIDTH = FACTOR // GROUPS
SLOTS = 4
LIMIT = 48 * 1024 * 1024

VMEM = pl.BlockSpec(memory_space=pltpu.VMEM)
SMEM = pl.BlockSpec(memory_space=pltpu.SMEM)
BF16 = jnp.bfloat16
F32 = jnp.float32


def tables():
    index = np.arange(FACTOR)
    angles = np.mod(index[:, None] * index[None, :], FACTOR) * (2.0 * math.pi / FACTOR)
    theta = index[:, None] * index[None, :] * (2.0 * math.pi / LEN)
    parts = [np.cos(angles), -np.sin(angles), np.cos(theta), -np.sin(theta)]
    return np.concatenate(parts).astype(np.float32)


def dot(a, b):
    return jnp.dot(a, b, preferred_element_type=F32)


def dot_t(a, b):
    return lax.dot_general(a, b, (((1,), (1,)), ((), ())), preferred_element_type=F32)


def front_kernel(taps_used, start, window, taps, x, tail, table, out, product, before):
    lane = lax.broadcasted_iota(jnp.int32, (1, FACTOR), 1)
    kept = jnp.where(lane < taps_used[0], taps[...], 0.0)
    kept = jnp.concatenate([kept, jnp.zeros_like(kept)], axis=1)
    spread = jnp.broadcast_to(kept, (2 * FACTOR, 2 * FACTOR))
    matrix = pltpu.roll(spread, FACTOR, 1, stride=1, stride_axis=0)[:, :FACTOR].astype(BF16)
    both = jnp.concatenate([matrix[FACTOR:], matrix[:FACTOR]], axis=1)
    before[...] = dot(tail[...], matrix[:FACTOR])
    first = table[: 2 * FACTOR].astype(BF16)
    low = lax.shift_right_logical(start[0], 7)
    row = lax.broadcasted_iota(jnp.int32, (8, FACTOR), 0)
    pick = (lax.broadcasted_iota(jnp.int32, (8, FACTOR), 1) == low + row).astype(F32).astype(BF16)
    cosine = dot(pick, first[:FACTOR])
    sine = dot(pick, first[FACTOR:])
    second = jnp.concatenate(
        [jnp.concatenate([cosine, -sine], axis=1), jnp.concatenate([sine, cosine], axis=1)], axis=0
    )
    second = (second * (1.0 / FACTOR)).astype(BF16)
    top = lax.broadcasted_iota(jnp.int32, (FACTOR, FACTOR), 0) == 0

    def some(i, carry):
        y = dot(x[pl.ds(BATCH * i, BATCH)].reshape(BATCH * FACTOR, FACTOR), both)
        parts = []
        for j in range(BATCH):
            now = y[j * FACTOR : (j + 1) * FACTOR]
            late = jnp.where(top, before[pl.ds(BATCH * i + j, 1), :], pltpu.roll(now[:, FACTOR:], 1, 0))
            parts.append((now[:, :FACTOR] + late).astype(BF16))
        section = dot(first, jnp.concatenate(parts, axis=1))
        halves = []
        for j in range(BATCH):
            re = section[:FACTOR, j * FACTOR : (j + 1) * FACTOR]
            im = section[FACTOR:, j * FACTOR : (j + 1) * FACTOR]
            twist_re = table[2 * FACTOR : 3 * FACTOR]
            twist_im = table[3 * FACTOR :]
            halves.append(
                jnp.concatenate([re * twist_re - im * twist_im, re * twist_im + im * twist_re], axis=1).astype(BF16)
            )
        got = dot_t(second, jnp.concatenate(halves, axis=0))
        for j in range(BATCH):
            product[:, pl.ds(BATCH * i + j, 1), :] = got[:, None, j * FACTOR : (j + 1) * FACTOR]
        return carry

    lax.fori_loop(0, COUNT // BATCH, some, 0)

    early = lax.broadcasted_iota(jnp.int32, (COUNT, FACTOR), 1) >= (start[0] & (FACTOR - 1))
    residue = lax.broadcasted_iota(jnp.int32, (FACTOR, BAND), 0)
    lane = lax.broadcasted_iota(jnp.int32, (FACTOR, BAND), 1)
    place = (lane & -FACTOR) + ((lane - WIDTH * window[0]) & (FACTOR - 1))
    placed = None
    for q in range(QUARTERS):
        re = jnp.where(early, product[q], product[q + 1])
        im = jnp.where(early, product[8 + q], product[9 + q])
        scale = lax.rsqrt(re * re + im * im + 1.0)
        white = jnp.concatenate([re * scale, im * scale], axis=0).astype(BF16)
        moved = dot(white, (place == QUARTERS * residue + q).astype(F32).astype(BF16))
        placed = moved if placed is None else placed + moved
    for z in range(4):
        for quarter in range(4):
            for o in range(2):
                at = o * COUNT + z * 8
                piece = placed[at : at + 8, quarter * FACTOR : (quarter + 1) * FACTOR]
                out[z * 8 + quarter * 2 + o] = piece.astype(BF16)


def pack_kernel(blocks, every, out):
    for i in range(COUNT):
        block = every[blocks[i]]
        for z in range(4):
            out[z * WINDOWS + i // 4, i % 4] = block
        for j in range(WINDOWS):
            out[i // 8 * WINDOWS + j, 4 + i % 8] = block


def turn_kernel(got, out):
    for i in range(COUNT):
        for r in range(8):
            out[r, i] = got[i, 4 + r]


M_STEP = 8


def spiral(parts, bits):
    for s in range(3):
        parts = [jnp.where(bits[s], parts[(a + (1 << s)) % GROUPS], parts[a]) for a in range(GROUPS)]
    return parts


def cross_kernel(parts, place, *refs):
    count = len(parts)
    mine, theirs, rows = refs[:count], refs[count : 2 * count], refs[2 * count]
    out, left, coef, mixed, stage, done = refs[-6:]
    x, core = place[0], place[1]
    spot = lax.broadcasted_iota(jnp.int32, (8, FACTOR), 1) // WIDTH
    bits = [(spot & (1 << s)) != 0 for s in range(3)]
    inner = lax.broadcasted_iota(jnp.int32, (WIDTH, FACTOR), 0)
    lane = lax.broadcasted_iota(jnp.int32, (WIDTH, FACTOR), 1)
    diagonal = inner == (lane & (WIDTH - 1))

    def cols(part, b, carry):
        for pair in range(2):
            tiles = []
            for half in range(2):
                d = 2 * pair + half
                whole = [[], []]
                for w in range(WINDOWS):
                    a = mine[part][d * WINDOWS + w, b].astype(F32)
                    t = theirs[part][d * WINDOWS + w, b].astype(F32)
                    whole[0].append(jnp.where(core == 0, a, t))
                    whole[1].append(jnp.where(core == 0, t, a))
                tiles.append([spiral(whole[i], bits) for i in range(2)])
            at = pl.multiple_of(b * 32 + pair * 16, 16)
            for g in range(GROUPS):
                for i in range(2):
                    packed = jnp.concatenate([tiles[h][i][-g % GROUPS] for h in range(2)], axis=0)
                    left[part, g, pl.ds(at, 16), i * FACTOR : (i + 1) * FACTOR] = packed.astype(BF16)
        return carry

    for part in range(count):
        lax.fori_loop(0, 4, functools.partial(cols, part), 0)

    def chunk_of(part):
        turn = jnp.int32(parts[0])
        for i in range(1, count):
            turn = jnp.where(part == i, parts[i], turn)
        return x ^ turn

    def prepare(step, slot):
        part = lax.shift_right_logical(step, 2)
        at = chunk_of(part) * 2
        z = step & 3
        for w in range(WINDOWS):
            for i in range(2):
                u = rows[at + i, z * WINDOWS + w].astype(F32)
                if w:
                    u = pltpu.roll(u, FACTOR - WIDTH * w, 1)
                u = pltpu.roll(u, 0, 1, stride=WIDTH, stride_axis=0)
                for s in range(3):
                    u = jnp.where(bits[s], pltpu.roll(u, 8 - (1 << s), 0), u)
                coef[slot, w, i] = u
                if i == 0:
                    coef[slot, w, 2] = -u

    def multiply(step, slot):
        part = lax.shift_right_logical(step, 2)
        for g in range(GROUPS):
            blocks = [
                [
                    jnp.where(diagonal, coef[slot, w, i, pl.ds(-g % GROUPS, 1), :], 0.0).astype(BF16)
                    for i in range(3)
                ]
                for w in range(WINDOWS)
            ]
            order = [blocks[(c - g) % GROUPS] for c in range(GROUPS)]
            top = jnp.concatenate([jnp.concatenate([k[0], k[1]], axis=1) for k in order], axis=0)
            low = jnp.concatenate([jnp.concatenate([k[1], k[2]], axis=1) for k in order], axis=0)
            mixed[slot, g] = dot(left[part, g], jnp.concatenate([top, low], axis=0))

    def copies(step):
        slot = step % SLOTS
        chunk = chunk_of(lax.shift_right_logical(step, 2))
        for o in range(2):
            lanes = pl.ds(pl.multiple_of((chunk + 4 * o) * FACTOR, FACTOR), FACTOR)
            yield pltpu.make_async_copy(
                stage.at[slot, o], out.at[pl.ds((step & 3) * M_STEP, M_STEP), :, lanes], done.at[slot, o]
            )

    def spread(slot, step):
        target = step % SLOTS
        for t in range(8):
            for o in range(2):
                halves = []
                for h in range(2):
                    lanes = slice(o * FACTOR, (o + 1) * FACTOR)
                    parts = [mixed[slot, g, 16 * t + 8 * h : 16 * t + 8 * h + 8, lanes] for g in range(GROUPS)]
                    halves.append(spiral(parts, bits))
                for m in range(M_STEP):
                    pair = [pltpu.roll(x[-m % GROUPS], FACTOR - WIDTH * m, 1) if m else x[0] for x in halves]
                    stage[target, o, m, 16 * t : 16 * t + 16, :] = jnp.concatenate(pair, axis=0).astype(BF16)

    steps = count * (COUNT // M_STEP)
    prepare(jnp.int32(0), 0)
    prepare(jnp.int32(1), 1)
    multiply(jnp.int32(0), 0)

    def both(i, carry):
        for slot in range(2):
            step = 2 * i + slot

            @pl.when(step >= SLOTS)
            def _():
                for copy in copies(step - SLOTS):
                    copy.wait()

            prepare(jnp.minimum(step + 2, steps - 1), slot)
            multiply(jnp.minimum(step + 1, steps - 1), 1 - slot)
            spread(slot, step)
            for copy in copies(step):
                copy.start()
        return carry

    lax.fori_loop(0, steps // 2, both, 0)
    for step in range(steps - SLOTS, steps):
        for copy in copies(jnp.int32(step)):
            copy.wait()


def cross(parts, place, mine, theirs, rows, before):
    args = [place, *mine, *theirs, rows]
    specs = [SMEM] + [VMEM] * (len(args) - 1)
    aliases = {}
    if before is not None:
        aliases = {len(args): 0}
        args.append(before)
        specs.append(pl.BlockSpec(memory_space=pl.ANY))
    return pl.pallas_call(
        functools.partial(cross_kernel, parts),
        in_specs=specs,
        out_specs=pl.BlockSpec(memory_space=pl.ANY),
        scratch_shapes=[
            pltpu.VMEM((len(parts), GROUPS, FACTOR, 2 * FACTOR), BF16),
            pltpu.VMEM((2, WINDOWS, 3, 8, FACTOR), F32),
            pltpu.VMEM((2, GROUPS, FACTOR, 2 * FACTOR), F32),
            pltpu.VMEM((SLOTS, 2, M_STEP, FACTOR, FACTOR), BF16),
            pltpu.SemaphoreType.DMA((SLOTS, 2)),
        ],
        out_shape=jax.ShapeDtypeStruct((COUNT, 128, 2 * BAND), BF16),
        input_output_aliases=aliases,
        compiler_params=pltpu.CompilerParams(vmem_limit_bytes=LIMIT),
    )(*args)


CHAN = ("z", "x", "c")
WIN = ("y", "h")


def shards(samples, fir_taps, tap_counts, band_start, grid_blocks):
    tail = lax.ppermute(samples[:, -FACTOR:], WIN, [(i, i + 1) for i in range(WINDOWS - 1)])
    pieces = pl.pallas_call(
        front_kernel,
        in_specs=[SMEM, SMEM, SMEM, VMEM, VMEM, VMEM, VMEM],
        out_specs=VMEM,
        out_shape=jax.ShapeDtypeStruct((COUNT, 8, FACTOR), BF16),
        scratch_shapes=[pltpu.VMEM((16, COUNT, FACTOR), F32), pltpu.VMEM((COUNT, FACTOR), F32)],
        compiler_params=pltpu.CompilerParams(vmem_limit_bytes=LIMIT),
    )(
        tap_counts,
        band_start,
        lax.axis_index(WIN).reshape(1),
        fir_taps.reshape(1, FACTOR),
        samples.reshape(COUNT, FACTOR, FACTOR),
        tail,
        tables(),
    )
    every = lax.all_to_all(pieces, CHAN, 0, 0, tiled=True)
    sent = pl.pallas_call(
        pack_kernel,
        in_specs=[SMEM, VMEM],
        out_specs=VMEM,
        out_shape=jax.ShapeDtypeStruct((COUNT, 12, 8, FACTOR), BF16),
    )(grid_blocks, every)
    got = lax.all_to_all(sent, ("z", *WIN), 0, 0, tiled=True)
    mine = [got[:, :4]]
    mine += [lax.ppermute(mine[0], "x", [(i, i ^ d) for i in range(4)]) for d in (1, 2, 3)]
    theirs = [lax.ppermute(this, "c", [(0, 1), (1, 0)]) for this in mine]
    rows = pl.pallas_call(
        turn_kernel,
        in_specs=[VMEM],
        out_specs=VMEM,
        out_shape=jax.ShapeDtypeStruct((8, COUNT, 8, FACTOR), BF16),
    )(got)
    rows = lax.all_to_all(rows, ("x", "c"), 0, 0, tiled=True)
    place = jnp.stack([lax.axis_index("x"), lax.axis_index("c")]).astype(jnp.int32)
    return cross((0, 1, 2, 3), place, mine, theirs, rows, None)


def solution(mesh):
    fine = jax.sharding.Mesh(mesh.devices.reshape(4, 4, 2, 4, 2), (*CHAN, *WIN))
    placed = (P(CHAN, WIN), P(), P(WIN), P(), P())
    return jax.shard_map(
        shards, mesh=fine, in_specs=placed, out_specs=P(CHAN, WIN, None), check_vma=False
    )
```

```python
import functools
import math

import jax
import jax.numpy as jnp
import numpy as np
from jax import lax
from jax.experimental import pallas as pl
from jax.experimental.pallas import tpu as pltpu
from jax.sharding import PartitionSpec as P

LEN = 16384
FACTOR = 128
BAND = 512
KMAX = 128
COUNT = 32
QUARTERS = BAND // FACTOR
WINDOWS = 8
BATCH = 8
GROUPS = 8
WIDTH = FACTOR // GROUPS
SLOTS = 4
LIMIT = 48 * 1024 * 1024
SMALL = pltpu.CompilerParams(vmem_limit_bytes=8 * 1024 * 1024)

VMEM = pl.BlockSpec(memory_space=pltpu.VMEM)
SMEM = pl.BlockSpec(memory_space=pltpu.SMEM)
BF16 = jnp.bfloat16
F32 = jnp.float32


def tables():
    index = np.arange(FACTOR)
    angles = np.mod(index[:, None] * index[None, :], FACTOR) * (2.0 * math.pi / FACTOR)
    theta = index[:, None] * index[None, :] * (2.0 * math.pi / LEN)
    parts = [np.cos(angles), -np.sin(angles), np.cos(theta), -np.sin(theta)]
    return np.concatenate(parts).astype(np.float32)


def dot(a, b):
    return jnp.dot(a, b, preferred_element_type=F32)


def dot_t(a, b):
    return lax.dot_general(a, b, (((1,), (1,)), ((), ())), preferred_element_type=F32)


def front_kernel(taps_used, start, window, taps, x, tail, table, out, product, before):
    lane = lax.broadcasted_iota(jnp.int32, (1, FACTOR), 1)
    kept = jnp.where(lane < taps_used[0], taps[...], 0.0)
    kept = jnp.concatenate([kept, jnp.zeros_like(kept)], axis=1)
    spread = jnp.broadcast_to(kept, (2 * FACTOR, 2 * FACTOR))
    matrix = pltpu.roll(spread, FACTOR, 1, stride=1, stride_axis=0)[:, :FACTOR].astype(BF16)
    both = jnp.concatenate([matrix[FACTOR:], matrix[:FACTOR]], axis=1)
    before[...] = dot(tail[...], matrix[:FACTOR])
    first = table[: 2 * FACTOR].astype(BF16)
    low = lax.shift_right_logical(start[0], 7)
    row = lax.broadcasted_iota(jnp.int32, (8, FACTOR), 0)
    pick = (lax.broadcasted_iota(jnp.int32, (8, FACTOR), 1) == low + row).astype(F32).astype(BF16)
    cosine = dot(pick, first[:FACTOR])
    sine = dot(pick, first[FACTOR:])
    second = jnp.concatenate(
        [jnp.concatenate([cosine, -sine], axis=1), jnp.concatenate([sine, cosine], axis=1)], axis=0
    )
    second = (second * (1.0 / FACTOR)).astype(BF16)
    top = lax.broadcasted_iota(jnp.int32, (FACTOR, FACTOR), 0) == 0

    def some(i, carry):
        y = dot(x[pl.ds(BATCH * i, BATCH)].reshape(BATCH * FACTOR, FACTOR), both)
        parts = []
        for j in range(BATCH):
            now = y[j * FACTOR : (j + 1) * FACTOR]
            late = jnp.where(top, before[pl.ds(BATCH * i + j, 1), :], pltpu.roll(now[:, FACTOR:], 1, 0))
            parts.append((now[:, :FACTOR] + late).astype(BF16))
        section = dot(first, jnp.concatenate(parts, axis=1))
        halves = []
        for j in range(BATCH):
            re = section[:FACTOR, j * FACTOR : (j + 1) * FACTOR]
            im = section[FACTOR:, j * FACTOR : (j + 1) * FACTOR]
            twist_re = table[2 * FACTOR : 3 * FACTOR]
            twist_im = table[3 * FACTOR :]
            halves.append(
                jnp.concatenate([re * twist_re - im * twist_im, re * twist_im + im * twist_re], axis=1).astype(BF16)
            )
        got = dot_t(second, jnp.concatenate(halves, axis=0))
        for j in range(BATCH):
            product[:, pl.ds(BATCH * i + j, 1), :] = got[:, None, j * FACTOR : (j + 1) * FACTOR]
        return carry

    lax.fori_loop(0, COUNT // BATCH, some, 0)

    early = lax.broadcasted_iota(jnp.int32, (COUNT, FACTOR), 1) >= (start[0] & (FACTOR - 1))
    residue = lax.broadcasted_iota(jnp.int32, (FACTOR, BAND), 0)
    lane = lax.broadcasted_iota(jnp.int32, (FACTOR, BAND), 1)
    place = (lane & -FACTOR) + ((lane - WIDTH * window[0]) & (FACTOR - 1))
    placed = None
    for q in range(QUARTERS):
        re = jnp.where(early, product[q], product[q + 1])
        im = jnp.where(early, product[8 + q], product[9 + q])
        scale = lax.rsqrt(re * re + im * im + 1.0)
        white = jnp.concatenate([re * scale, im * scale], axis=0).astype(BF16)
        moved = dot(white, (place == QUARTERS * residue + q).astype(F32).astype(BF16))
        placed = moved if placed is None else placed + moved
    for z in range(4):
        for quarter in range(4):
            for o in range(2):
                at = o * COUNT + z * 8
                piece = placed[at : at + 8, quarter * FACTOR : (quarter + 1) * FACTOR]
                out[z * 8 + quarter * 2 + o] = piece.astype(BF16)


def pack_kernel(blocks, every, out):
    for i in range(COUNT):
        block = every[blocks[i]]
        for z in range(4):
            out[z * WINDOWS + i // 4, i % 4] = block
        for j in range(WINDOWS):
            out[i // 8 * WINDOWS + j, 4 + i % 8] = block


def turn_kernel(got, out):
    for i in range(COUNT):
        for r in range(8):
            out[r, i] = got[i, 4 + r]


M_STEP = 8


def spiral(parts, bits):
    for s in range(3):
        parts = [jnp.where(bits[s], parts[(a + (1 << s)) % GROUPS], parts[a]) for a in range(GROUPS)]
    return parts


def cross_kernel(parts, chunk_at, core_at, *refs):
    count = len(parts)
    mine, theirs, rows = refs[:count], refs[count : 2 * count], refs[2 * count]
    out, left, coef, mixed, stage, done = refs[-6:]
    x, core = chunk_at[0], core_at[0]
    spot = lax.broadcasted_iota(jnp.int32, (8, FACTOR), 1) // WIDTH
    bits = [(spot & (1 << s)) != 0 for s in range(3)]
    inner = lax.broadcasted_iota(jnp.int32, (WIDTH, FACTOR), 0)
    lane = lax.broadcasted_iota(jnp.int32, (WIDTH, FACTOR), 1)
    diagonal = inner == (lane & (WIDTH - 1))

    def cols(part, b, carry):
        for pair in range(2):
            tiles = []
            for half in range(2):
                d = 2 * pair + half
                whole = [[], []]
                for w in range(WINDOWS):
                    a = mine[part][d * WINDOWS + w, b].astype(F32)
                    t = theirs[part][d * WINDOWS + w, b].astype(F32)
                    whole[0].append(jnp.where(core == 0, a, t))
                    whole[1].append(jnp.where(core == 0, t, a))
                tiles.append([spiral(whole[i], bits) for i in range(2)])
            at = pl.multiple_of(b * 32 + pair * 16, 16)
            for g in range(GROUPS):
                for i in range(2):
                    packed = jnp.concatenate([tiles[h][i][-g % GROUPS] for h in range(2)], axis=0)
                    left[part, g, pl.ds(at, 16), i * FACTOR : (i + 1) * FACTOR] = packed.astype(BF16)
        return carry

    for part in range(count):
        lax.fori_loop(0, 4, functools.partial(cols, part), 0)

    def chunk_of(part):
        turn = jnp.int32(parts[0])
        for i in range(1, count):
            turn = jnp.where(part == i, parts[i], turn)
        return x ^ turn

    def prepare(step, slot):
        part = lax.shift_right_logical(step, 2)
        at = chunk_of(part) * 2
        z = step & 3
        for w in range(WINDOWS):
            for i in range(2):
                u = rows[at + i, z * WINDOWS + w].astype(F32)
                if w:
                    u = pltpu.roll(u, FACTOR - WIDTH * w, 1)
                u = pltpu.roll(u, 0, 1, stride=WIDTH, stride_axis=0)
                for s in range(3):
                    u = jnp.where(bits[s], pltpu.roll(u, 8 - (1 << s), 0), u)
                coef[slot, w, i] = u
                if i == 0:
                    coef[slot, w, 2] = -u

    def multiply(step, slot):
        part = lax.shift_right_logical(step, 2)
        for g in range(GROUPS):
            blocks = [
                [
                    jnp.where(diagonal, coef[slot, w, i, pl.ds(-g % GROUPS, 1), :], 0.0).astype(BF16)
                    for i in range(3)
                ]
                for w in range(WINDOWS)
            ]
            order = [blocks[(c - g) % GROUPS] for c in range(GROUPS)]
            top = jnp.concatenate([jnp.concatenate([k[0], k[1]], axis=1) for k in order], axis=0)
            low = jnp.concatenate([jnp.concatenate([k[1], k[2]], axis=1) for k in order], axis=0)
            mixed[slot, g] = dot(left[part, g], jnp.concatenate([top, low], axis=0))

    def copies(step):
        slot = step % SLOTS
        chunk = chunk_of(lax.shift_right_logical(step, 2))
        for o in range(2):
            lanes = pl.ds(pl.multiple_of((chunk + 4 * o) * FACTOR, FACTOR), FACTOR)
            yield pltpu.make_async_copy(
                stage.at[slot, o], out.at[pl.ds((step & 3) * M_STEP, M_STEP), :, lanes], done.at[slot, o]
            )

    def spread(slot, step):
        target = step % SLOTS
        for t in range(8):
            for o in range(2):
                halves = []
                for h in range(2):
                    lanes = slice(o * FACTOR, (o + 1) * FACTOR)
                    parts = [mixed[slot, g, 16 * t + 8 * h : 16 * t + 8 * h + 8, lanes] for g in range(GROUPS)]
                    halves.append(spiral(parts, bits))
                for m in range(M_STEP):
                    pair = [pltpu.roll(x[-m % GROUPS], FACTOR - WIDTH * m, 1) if m else x[0] for x in halves]
                    stage[target, o, m, 16 * t : 16 * t + 16, :] = jnp.concatenate(pair, axis=0).astype(BF16)

    steps = count * (COUNT // M_STEP)
    prepare(jnp.int32(0), 0)
    prepare(jnp.int32(1), 1)
    multiply(jnp.int32(0), 0)

    def both(i, carry):
        for slot in range(2):
            step = 2 * i + slot

            @pl.when(step >= SLOTS)
            def _():
                for copy in copies(step - SLOTS):
                    copy.wait()

            prepare(jnp.minimum(step + 2, steps - 1), slot)
            multiply(jnp.minimum(step + 1, steps - 1), 1 - slot)
            spread(slot, step)
            for copy in copies(step):
                copy.start()
        return carry

    lax.fori_loop(0, steps // 2, both, 0)
    for step in range(steps - SLOTS, steps):
        for copy in copies(jnp.int32(step)):
            copy.wait()


def cross(parts, chunk_at, core_at, mine, theirs, rows, before):
    args = [chunk_at, core_at, *mine, *theirs, rows]
    specs = [SMEM] * 2 + [VMEM] * (len(args) - 2)
    aliases = {}
    if before is not None:
        aliases = {len(args): 0}
        args.append(before)
        specs.append(pl.BlockSpec(memory_space=pl.ANY))
    return pl.pallas_call(
        functools.partial(cross_kernel, parts),
        in_specs=specs,
        out_specs=pl.BlockSpec(memory_space=pl.ANY),
        scratch_shapes=[
            pltpu.VMEM((len(parts), GROUPS, FACTOR, 2 * FACTOR), BF16),
            pltpu.VMEM((2, WINDOWS, 3, 8, FACTOR), F32),
            pltpu.VMEM((2, GROUPS, FACTOR, 2 * FACTOR), F32),
            pltpu.VMEM((SLOTS, 2, M_STEP, FACTOR, FACTOR), BF16),
            pltpu.SemaphoreType.DMA((SLOTS, 2)),
        ],
        out_shape=jax.ShapeDtypeStruct((COUNT, 128, 2 * BAND), BF16),
        input_output_aliases=aliases,
        compiler_params=pltpu.CompilerParams(vmem_limit_bytes=LIMIT),
    )(*args)


CHAN = ("z", "x", "c")
WIN = ("y", "h")


def shards(samples, fir_taps, tap_counts, band_start, grid_blocks):
    tail = lax.ppermute(samples[:, -FACTOR:], WIN, [(i, i + 1) for i in range(WINDOWS - 1)])
    pieces = pl.pallas_call(
        front_kernel,
        in_specs=[SMEM, SMEM, SMEM, VMEM, VMEM, VMEM, VMEM],
        out_specs=VMEM,
        out_shape=jax.ShapeDtypeStruct((COUNT, 8, FACTOR), BF16),
        scratch_shapes=[pltpu.VMEM((16, COUNT, FACTOR), F32), pltpu.VMEM((COUNT, FACTOR), F32)],
        compiler_params=pltpu.CompilerParams(vmem_limit_bytes=LIMIT),
    )(
        tap_counts,
        band_start,
        lax.axis_index(WIN).reshape(1),
        fir_taps.reshape(1, FACTOR),
        samples.reshape(COUNT, FACTOR, FACTOR),
        tail,
        tables(),
    )
    every = lax.all_to_all(pieces, CHAN, 0, 0, tiled=True)
    sent = pl.pallas_call(
        pack_kernel,
        in_specs=[SMEM, VMEM],
        out_specs=VMEM,
        out_shape=jax.ShapeDtypeStruct((COUNT, 12, 8, FACTOR), BF16),
        compiler_params=SMALL,
    )(grid_blocks, every)
    got = lax.all_to_all(sent, ("z", *WIN), 0, 0, tiled=True)
    mine = [got[:, :4]]
    mine += [lax.ppermute(mine[0], "x", [(i, i ^ d) for i in range(4)]) for d in (1, 2, 3)]
    theirs = [lax.ppermute(this, "c", [(0, 1), (1, 0)]) for this in mine]
    rows = pl.pallas_call(
        turn_kernel,
        in_specs=[VMEM],
        out_specs=VMEM,
        out_shape=jax.ShapeDtypeStruct((8, COUNT, 8, FACTOR), BF16),
        compiler_params=SMALL,
    )(got)
    rows = lax.all_to_all(rows, ("x", "c"), 0, 0, tiled=True)
    chunk_at, core_at = lax.axis_index("x").reshape(1), lax.axis_index("c").reshape(1)
    return cross((0, 1, 2, 3), chunk_at, core_at, mine, theirs, rows, None)


def solution(mesh):
    fine = jax.sharding.Mesh(mesh.devices.reshape(4, 4, 2, 4, 2), (*CHAN, *WIN))
    placed = (P(CHAN, WIN), P(), P(WIN), P(), P())
    return jax.shard_map(
        shards, mesh=fine, in_specs=placed, out_specs=P(CHAN, WIN, None), check_vma=False
    )
```

```python
import functools
import math

import jax
import jax.numpy as jnp
import numpy as np
from jax import lax
from jax.experimental import pallas as pl
from jax.experimental.pallas import tpu as pltpu
from jax.sharding import PartitionSpec as P

LEN = 16384
FACTOR = 128
BAND = 512
KMAX = 128
COUNT = 32
QUARTERS = BAND // FACTOR
WINDOWS = 8
BATCH = 8
GROUPS = 8
WIDTH = FACTOR // GROUPS
SLOTS = 4
LIMIT = 48 * 1024 * 1024
SMALL = pltpu.CompilerParams(vmem_limit_bytes=8 * 1024 * 1024)

VMEM = pl.BlockSpec(memory_space=pltpu.VMEM)
SMEM = pl.BlockSpec(memory_space=pltpu.SMEM)
BF16 = jnp.bfloat16
F32 = jnp.float32


def tables():
    index = np.arange(FACTOR)
    angles = np.mod(index[:, None] * index[None, :], FACTOR) * (2.0 * math.pi / FACTOR)
    theta = index[:, None] * index[None, :] * (2.0 * math.pi / LEN)
    parts = [np.cos(angles), -np.sin(angles), np.cos(theta), -np.sin(theta)]
    return np.concatenate(parts).astype(np.float32)


def dot(a, b):
    return jnp.dot(a, b, preferred_element_type=F32)


def dot_t(a, b):
    return lax.dot_general(a, b, (((1,), (1,)), ((), ())), preferred_element_type=F32)


def front_kernel(settings, x, tail, table, out, product, before):
    window = lax.axis_index("y") * 2 + lax.axis_index("h")
    lane = lax.broadcasted_iota(jnp.int32, (1, FACTOR), 1)
    used = jnp.broadcast_to(settings[:, FACTOR : FACTOR + 1], (1, FACTOR)).astype(jnp.int32)
    start = jnp.broadcast_to(settings[:, FACTOR + 1 : FACTOR + 2], (1, FACTOR)).astype(jnp.int32)
    kept = jnp.where(lane < used, settings[:, :FACTOR], 0.0)
    kept = jnp.concatenate([kept, jnp.zeros_like(kept)], axis=1)
    spread = jnp.broadcast_to(kept, (2 * FACTOR, 2 * FACTOR))
    matrix = pltpu.roll(spread, FACTOR, 1, stride=1, stride_axis=0)[:, :FACTOR].astype(BF16)
    both = jnp.concatenate([matrix[FACTOR:], matrix[:FACTOR]], axis=1)
    before[...] = dot(tail[...], matrix[:FACTOR])
    first = table[: 2 * FACTOR].astype(BF16)
    low = lax.shift_right_logical(start, 7)
    row = lax.broadcasted_iota(jnp.int32, (8, FACTOR), 0)
    pick = (lax.broadcasted_iota(jnp.int32, (8, FACTOR), 1) == low + row).astype(F32).astype(BF16)
    cosine = dot(pick, first[:FACTOR])
    sine = dot(pick, first[FACTOR:])
    second = jnp.concatenate(
        [jnp.concatenate([cosine, -sine], axis=1), jnp.concatenate([sine, cosine], axis=1)], axis=0
    )
    second = (second * (1.0 / FACTOR)).astype(BF16)
    top = lax.broadcasted_iota(jnp.int32, (FACTOR, FACTOR), 0) == 0

    def some(i, carry):
        y = dot(x[pl.ds(BATCH * i, BATCH)].reshape(BATCH * FACTOR, FACTOR), both)
        parts = []
        for j in range(BATCH):
            now = y[j * FACTOR : (j + 1) * FACTOR]
            late = jnp.where(top, before[pl.ds(BATCH * i + j, 1), :], pltpu.roll(now[:, FACTOR:], 1, 0))
            parts.append((now[:, :FACTOR] + late).astype(BF16))
        section = dot(first, jnp.concatenate(parts, axis=1))
        halves = []
        for j in range(BATCH):
            re = section[:FACTOR, j * FACTOR : (j + 1) * FACTOR]
            im = section[FACTOR:, j * FACTOR : (j + 1) * FACTOR]
            twist_re = table[2 * FACTOR : 3 * FACTOR]
            twist_im = table[3 * FACTOR :]
            halves.append(
                jnp.concatenate([re * twist_re - im * twist_im, re * twist_im + im * twist_re], axis=1).astype(BF16)
            )
        got = dot_t(second, jnp.concatenate(halves, axis=0))
        for j in range(BATCH):
            product[:, pl.ds(BATCH * i + j, 1), :] = got[:, None, j * FACTOR : (j + 1) * FACTOR]
        return carry

    lax.fori_loop(0, COUNT // BATCH, some, 0)

    early = lax.broadcasted_iota(jnp.int32, (COUNT, FACTOR), 1) >= (start & (FACTOR - 1))
    residue = lax.broadcasted_iota(jnp.int32, (FACTOR, BAND), 0)
    lane = lax.broadcasted_iota(jnp.int32, (FACTOR, BAND), 1)
    place = (lane & -FACTOR) + ((lane - WIDTH * window) & (FACTOR - 1))
    placed = None
    for q in range(QUARTERS):
        re = jnp.where(early, product[q], product[q + 1])
        im = jnp.where(early, product[8 + q], product[9 + q])
        scale = lax.rsqrt(re * re + im * im + 1.0)
        white = jnp.concatenate([re * scale, im * scale], axis=0).astype(BF16)
        moved = dot(white, (place == QUARTERS * residue + q).astype(F32).astype(BF16))
        placed = moved if placed is None else placed + moved
    for z in range(4):
        for quarter in range(4):
            for o in range(2):
                at = o * COUNT + z * 8
                piece = placed[at : at + 8, quarter * FACTOR : (quarter + 1) * FACTOR]
                out[z * 8 + quarter * 2 + o] = piece.astype(BF16)


def pack_kernel(blocks, every, out):
    for i in range(COUNT):
        block = every[blocks[i]]
        for z in range(4):
            out[z * WINDOWS + i // 4, i % 4] = block
        for j in range(WINDOWS):
            out[i // 8 * WINDOWS + j, 4 + i % 8] = block


def turn_kernel(got, out):
    for i in range(COUNT):
        for r in range(8):
            out[r, i] = got[i, 4 + r]


M_STEP = 8


def spiral(parts, bits):
    for s in range(3):
        parts = [jnp.where(bits[s], parts[(a + (1 << s)) % GROUPS], parts[a]) for a in range(GROUPS)]
    return parts


def cross_kernel(parts, *refs):
    count = len(parts)
    mine, theirs, rows = refs[:count], refs[count : 2 * count], refs[2 * count]
    out, left, coef, mixed, stage, done = refs[-6:]
    x, core = lax.axis_index("x"), lax.axis_index("c")
    spot = lax.broadcasted_iota(jnp.int32, (8, FACTOR), 1) // WIDTH
    bits = [(spot & (1 << s)) != 0 for s in range(3)]
    inner = lax.broadcasted_iota(jnp.int32, (WIDTH, FACTOR), 0)
    lane = lax.broadcasted_iota(jnp.int32, (WIDTH, FACTOR), 1)
    diagonal = inner == (lane & (WIDTH - 1))

    def cols(part, b, carry):
        for pair in range(2):
            tiles = []
            for half in range(2):
                d = 2 * pair + half
                whole = [[], []]
                for w in range(WINDOWS):
                    a = mine[part][d * WINDOWS + w, b].astype(F32)
                    t = theirs[part][d * WINDOWS + w, b].astype(F32)
                    whole[0].append(jnp.where(core == 0, a, t))
                    whole[1].append(jnp.where(core == 0, t, a))
                tiles.append([spiral(whole[i], bits) for i in range(2)])
            at = pl.multiple_of(b * 32 + pair * 16, 16)
            for g in range(GROUPS):
                for i in range(2):
                    packed = jnp.concatenate([tiles[h][i][-g % GROUPS] for h in range(2)], axis=0)
                    left[part, g, pl.ds(at, 16), i * FACTOR : (i + 1) * FACTOR] = packed.astype(BF16)
        return carry

    for part in range(count):
        lax.fori_loop(0, 4, functools.partial(cols, part), 0)

    def chunk_of(part):
        turn = jnp.int32(parts[0])
        for i in range(1, count):
            turn = jnp.where(part == i, parts[i], turn)
        return x ^ turn

    def prepare(step, slot):
        part = lax.shift_right_logical(step, 2)
        at = chunk_of(part) * 2
        z = step & 3
        for w in range(WINDOWS):
            for i in range(2):
                u = rows[at + i, z * WINDOWS + w].astype(F32)
                if w:
                    u = pltpu.roll(u, FACTOR - WIDTH * w, 1)
                u = pltpu.roll(u, 0, 1, stride=WIDTH, stride_axis=0)
                for s in range(3):
                    u = jnp.where(bits[s], pltpu.roll(u, 8 - (1 << s), 0), u)
                coef[slot, w, i] = u
                if i == 0:
                    coef[slot, w, 2] = -u

    def multiply(step, slot):
        part = lax.shift_right_logical(step, 2)
        for g in range(GROUPS):
            blocks = [
                [
                    jnp.where(diagonal, coef[slot, w, i, pl.ds(-g % GROUPS, 1), :], 0.0).astype(BF16)
                    for i in range(3)
                ]
                for w in range(WINDOWS)
            ]
            order = [blocks[(c - g) % GROUPS] for c in range(GROUPS)]
            top = jnp.concatenate([jnp.concatenate([k[0], k[1]], axis=1) for k in order], axis=0)
            low = jnp.concatenate([jnp.concatenate([k[1], k[2]], axis=1) for k in order], axis=0)
            mixed[slot, g] = dot(left[part, g], jnp.concatenate([top, low], axis=0))

    def copies(step):
        slot = step % SLOTS
        chunk = chunk_of(lax.shift_right_logical(step, 2))
        for o in range(2):
            lanes = pl.ds(pl.multiple_of((chunk + 4 * o) * FACTOR, FACTOR), FACTOR)
            yield pltpu.make_async_copy(
                stage.at[slot, o], out.at[pl.ds((step & 3) * M_STEP, M_STEP), :, lanes], done.at[slot, o]
            )

    def spread(slot, step):
        target = step % SLOTS
        for t in range(8):
            for o in range(2):
                halves = []
                for h in range(2):
                    lanes = slice(o * FACTOR, (o + 1) * FACTOR)
                    parts = [mixed[slot, g, 16 * t + 8 * h : 16 * t + 8 * h + 8, lanes] for g in range(GROUPS)]
                    halves.append(spiral(parts, bits))
                for m in range(M_STEP):
                    pair = [pltpu.roll(x[-m % GROUPS], FACTOR - WIDTH * m, 1) if m else x[0] for x in halves]
                    stage[target, o, m, 16 * t : 16 * t + 16, :] = jnp.concatenate(pair, axis=0).astype(BF16)

    steps = count * (COUNT // M_STEP)
    prepare(jnp.int32(0), 0)
    prepare(jnp.int32(1), 1)
    multiply(jnp.int32(0), 0)

    def both(i, carry):
        for slot in range(2):
            step = 2 * i + slot

            @pl.when(step >= SLOTS)
            def _():
                for copy in copies(step - SLOTS):
                    copy.wait()

            prepare(jnp.minimum(step + 2, steps - 1), slot)
            multiply(jnp.minimum(step + 1, steps - 1), 1 - slot)
            spread(slot, step)
            for copy in copies(step):
                copy.start()
        return carry

    lax.fori_loop(0, steps // 2, both, 0)
    for step in range(steps - SLOTS, steps):
        for copy in copies(jnp.int32(step)):
            copy.wait()


def cross(parts, mine, theirs, rows, before):
    args = [*mine, *theirs, rows]
    specs = [VMEM] * len(args)
    aliases = {}
    if before is not None:
        aliases = {len(args): 0}
        args.append(before)
        specs.append(pl.BlockSpec(memory_space=pl.ANY))
    return pl.pallas_call(
        functools.partial(cross_kernel, parts),
        in_specs=specs,
        out_specs=pl.BlockSpec(memory_space=pl.ANY),
        scratch_shapes=[
            pltpu.VMEM((len(parts), GROUPS, FACTOR, 2 * FACTOR), BF16),
            pltpu.VMEM((2, WINDOWS, 3, 8, FACTOR), F32),
            pltpu.VMEM((2, GROUPS, FACTOR, 2 * FACTOR), F32),
            pltpu.VMEM((SLOTS, 2, M_STEP, FACTOR, FACTOR), BF16),
            pltpu.SemaphoreType.DMA((SLOTS, 2)),
        ],
        out_shape=jax.ShapeDtypeStruct((COUNT, 128, 2 * BAND), BF16),
        input_output_aliases=aliases,
        compiler_params=pltpu.CompilerParams(vmem_limit_bytes=LIMIT),
    )(*args)


CHAN = ("z", "x", "c")
WIN = ("y", "h")


def shards(samples, fir_taps, tap_counts, band_start, grid_blocks):
    tail = lax.ppermute(samples[:, -FACTOR:], WIN, [(i, i + 1) for i in range(WINDOWS - 1)])
    settings = jnp.concatenate(
        [fir_taps, tap_counts.astype(F32), band_start.astype(F32), jnp.zeros((FACTOR - 2,), F32)]
    )
    pieces = pl.pallas_call(
        front_kernel,
        in_specs=[VMEM, VMEM, VMEM, VMEM],
        out_specs=VMEM,
        out_shape=jax.ShapeDtypeStruct((COUNT, 8, FACTOR), BF16),
        scratch_shapes=[pltpu.VMEM((16, COUNT, FACTOR), F32), pltpu.VMEM((COUNT, FACTOR), F32)],
        compiler_params=pltpu.CompilerParams(vmem_limit_bytes=LIMIT),
    )(
        settings.reshape(1, 2 * FACTOR),
        samples.reshape(COUNT, FACTOR, FACTOR),
        tail,
        tables(),
    )
    every = lax.all_to_all(pieces, CHAN, 0, 0, tiled=True)
    sent = pl.pallas_call(
        pack_kernel,
        in_specs=[SMEM, VMEM],
        out_specs=VMEM,
        out_shape=jax.ShapeDtypeStruct((COUNT, 12, 8, FACTOR), BF16),
        compiler_params=SMALL,
    )(grid_blocks, every)
    got = lax.all_to_all(sent, ("z", *WIN), 0, 0, tiled=True)
    mine = [got[:, :4]]
    mine += [lax.ppermute(mine[0], "x", [(i, i ^ d) for i in range(4)]) for d in (1, 2, 3)]
    theirs = [lax.ppermute(this, "c", [(0, 1), (1, 0)]) for this in mine]
    rows = pl.pallas_call(
        turn_kernel,
        in_specs=[VMEM],
        out_specs=VMEM,
        out_shape=jax.ShapeDtypeStruct((8, COUNT, 8, FACTOR), BF16),
        compiler_params=SMALL,
    )(got)
    rows = lax.all_to_all(rows, ("x", "c"), 0, 0, tiled=True)
    return cross((0, 1, 2, 3), mine, theirs, rows, None)


def solution(mesh):
    fine = jax.sharding.Mesh(mesh.devices.reshape(4, 4, 2, 4, 2), (*CHAN, *WIN))
    placed = (P(CHAN, WIN), P(), P(WIN), P(), P())
    return jax.shard_map(
        shards, mesh=fine, in_specs=placed, out_specs=P(CHAN, WIN, None), check_vma=False
    )
```

```python
import functools
import math

import jax
import jax.numpy as jnp
import numpy as np
from jax import lax
from jax.experimental import pallas as pl
from jax.experimental.pallas import tpu as pltpu
from jax.sharding import PartitionSpec as P

LEN = 16384
FACTOR = 128
BAND = 512
KMAX = 128
COUNT = 32
QUARTERS = BAND // FACTOR
WINDOWS = 8
BATCH = 8
GROUPS = 8
WIDTH = FACTOR // GROUPS
SLOTS = 4
LIMIT = 48 * 1024 * 1024
SMALL = pltpu.CompilerParams(vmem_limit_bytes=8 * 1024 * 1024)

VMEM = pl.BlockSpec(memory_space=pltpu.VMEM)
SMEM = pl.BlockSpec(memory_space=pltpu.SMEM)
BF16 = jnp.bfloat16
F32 = jnp.float32


def tables():
    index = np.arange(FACTOR)
    angles = np.mod(index[:, None] * index[None, :], FACTOR) * (2.0 * math.pi / FACTOR)
    theta = index[:, None] * index[None, :] * (2.0 * math.pi / LEN)
    parts = [np.cos(angles), -np.sin(angles), np.cos(theta), -np.sin(theta)]
    return np.concatenate(parts).astype(np.float32)


def dot(a, b):
    return jnp.dot(a, b, preferred_element_type=F32)


def dot_t(a, b):
    return lax.dot_general(a, b, (((1,), (1,)), ((), ())), preferred_element_type=F32)


def front_kernel(settings, x, tail, table, out, product, before):
    window = lax.axis_index("y") * 2 + lax.axis_index("h")
    lane = lax.broadcasted_iota(jnp.int32, (1, FACTOR), 1)
    used = jnp.broadcast_to(settings[:, FACTOR : FACTOR + 1], (1, FACTOR)).astype(jnp.int32)
    start = jnp.broadcast_to(settings[:, FACTOR + 1 : FACTOR + 2], (1, FACTOR)).astype(jnp.int32)
    kept = jnp.where(lane < used, settings[:, :FACTOR], 0.0)
    kept = jnp.concatenate([kept, jnp.zeros_like(kept)], axis=1)
    spread = jnp.broadcast_to(kept, (2 * FACTOR, 2 * FACTOR))
    matrix = pltpu.roll(spread, FACTOR, 1, stride=1, stride_axis=0)[:, :FACTOR].astype(BF16)
    both = jnp.concatenate([matrix[FACTOR:], matrix[:FACTOR]], axis=1)
    before[...] = dot(tail[...], matrix[:FACTOR])
    first = table[: 2 * FACTOR].astype(BF16)
    low = lax.shift_right_logical(start, 7)
    row = lax.broadcasted_iota(jnp.int32, (8, FACTOR), 0)
    pick = (lax.broadcasted_iota(jnp.int32, (8, FACTOR), 1) == low + row).astype(F32).astype(BF16)
    cosine = dot(pick, first[:FACTOR])
    sine = dot(pick, first[FACTOR:])
    second = jnp.concatenate(
        [jnp.concatenate([cosine, -sine], axis=1), jnp.concatenate([sine, cosine], axis=1)], axis=0
    )
    second = (second * (1.0 / FACTOR)).astype(BF16)
    top = lax.broadcasted_iota(jnp.int32, (FACTOR, FACTOR), 0) == 0

    def some(i, carry):
        y = dot(x[pl.ds(BATCH * i, BATCH)].reshape(BATCH * FACTOR, FACTOR), both)
        parts = []
        for j in range(BATCH):
            now = y[j * FACTOR : (j + 1) * FACTOR]
            late = jnp.where(top, before[pl.ds(BATCH * i + j, 1), :], pltpu.roll(now[:, FACTOR:], 1, 0))
            parts.append((now[:, :FACTOR] + late).astype(BF16))
        section = dot(first, jnp.concatenate(parts, axis=1))
        halves = []
        for j in range(BATCH):
            re = section[:FACTOR, j * FACTOR : (j + 1) * FACTOR]
            im = section[FACTOR:, j * FACTOR : (j + 1) * FACTOR]
            twist_re = table[2 * FACTOR : 3 * FACTOR]
            twist_im = table[3 * FACTOR :]
            halves.append(
                jnp.concatenate([re * twist_re - im * twist_im, re * twist_im + im * twist_re], axis=1).astype(BF16)
            )
        got = dot_t(second, jnp.concatenate(halves, axis=0))
        for j in range(BATCH):
            product[:, pl.ds(BATCH * i + j, 1), :] = got[:, None, j * FACTOR : (j + 1) * FACTOR]
        return carry

    lax.fori_loop(0, COUNT // BATCH, some, 0)

    early = lax.broadcasted_iota(jnp.int32, (COUNT, FACTOR), 1) >= (start & (FACTOR - 1))
    residue = lax.broadcasted_iota(jnp.int32, (FACTOR, BAND), 0)
    lane = lax.broadcasted_iota(jnp.int32, (FACTOR, BAND), 1)
    place = (lane & -FACTOR) + ((lane - WIDTH * window) & (FACTOR - 1))
    placed = None
    for q in range(QUARTERS):
        re = jnp.where(early, product[q], product[q + 1])
        im = jnp.where(early, product[8 + q], product[9 + q])
        scale = lax.rsqrt(re * re + im * im + 1.0)
        white = jnp.concatenate([re * scale, im * scale], axis=0).astype(BF16)
        moved = dot(white, (place == QUARTERS * residue + q).astype(F32).astype(BF16))
        placed = moved if placed is None else placed + moved
    for z in range(4):
        for quarter in range(4):
            for o in range(2):
                at = o * COUNT + z * 8
                piece = placed[at : at + 8, quarter * FACTOR : (quarter + 1) * FACTOR]
                out[z * 8 + quarter * 2 + o] = piece.astype(BF16)


def pack_kernel(blocks, every, out):
    for i in range(COUNT):
        block = every[blocks[i]]
        for z in range(4):
            out[z * WINDOWS + i // 4, i % 4] = block
        for j in range(WINDOWS):
            out[i // 8 * WINDOWS + j, 4 + i % 8] = block


def turn_kernel(got, out):
    for i in range(COUNT):
        for r in range(8):
            out[r, i] = got[i, 4 + r]


M_STEP = 8


def spiral(parts, bits):
    for s in range(3):
        parts = [jnp.where(bits[s], parts[(a + (1 << s)) % GROUPS], parts[a]) for a in range(GROUPS)]
    return parts


def cross_kernel(parts, *refs):
    count = len(parts)
    mine, theirs, rows = refs[:count], refs[count : 2 * count], refs[2 * count]
    out, left, coef, mixed, stage, done = refs[-6:]
    x, core = lax.axis_index("x"), lax.axis_index("c")
    spot = lax.broadcasted_iota(jnp.int32, (8, FACTOR), 1) // WIDTH
    bits = [(spot & (1 << s)) != 0 for s in range(3)]
    inner = lax.broadcasted_iota(jnp.int32, (WIDTH, FACTOR), 0)
    lane = lax.broadcasted_iota(jnp.int32, (WIDTH, FACTOR), 1)
    diagonal = inner == (lane & (WIDTH - 1))

    def cols(part, b, carry):
        for pair in range(2):
            tiles = []
            for half in range(2):
                d = 2 * pair + half
                whole = [[], []]
                for w in range(WINDOWS):
                    a = mine[part][d * WINDOWS + w, b].astype(F32)
                    t = theirs[part][d * WINDOWS + w, b].astype(F32)
                    whole[0].append(jnp.where(core == 0, a, t))
                    whole[1].append(jnp.where(core == 0, t, a))
                tiles.append([spiral(whole[i], bits) for i in range(2)])
            at = pl.multiple_of(b * 32 + pair * 16, 16)
            for g in range(GROUPS):
                for i in range(2):
                    packed = jnp.concatenate([tiles[h][i][-g % GROUPS] for h in range(2)], axis=0)
                    left[part, g, pl.ds(at, 16), i * FACTOR : (i + 1) * FACTOR] = packed.astype(BF16)
        return carry

    for part in range(count):
        lax.fori_loop(0, 4, functools.partial(cols, part), 0)

    def chunk_of(part):
        turn = jnp.int32(parts[0])
        for i in range(1, count):
            turn = jnp.where(part == i, parts[i], turn)
        return x ^ turn

    def prepare(step, slot):
        part = lax.shift_right_logical(step, 2)
        at = chunk_of(part) * 2
        z = step & 3
        for w in range(WINDOWS):
            for i in range(2):
                u = rows[at + i, z * WINDOWS + w].astype(F32)
                if w:
                    u = pltpu.roll(u, FACTOR - WIDTH * w, 1)
                u = pltpu.roll(u, 0, 1, stride=WIDTH, stride_axis=0)
                for s in range(3):
                    u = jnp.where(bits[s], pltpu.roll(u, 8 - (1 << s), 0), u)
                coef[slot, w, i] = u
                if i == 0:
                    coef[slot, w, 2] = -u

    def multiply(step, slot):
        part = lax.shift_right_logical(step, 2)
        for g in range(GROUPS):
            blocks = [
                [
                    jnp.where(diagonal, coef[slot, w, i, pl.ds(-g % GROUPS, 1), :], 0.0).astype(BF16)
                    for i in range(3)
                ]
                for w in range(WINDOWS)
            ]
            order = [blocks[(c - g) % GROUPS] for c in range(GROUPS)]
            top = jnp.concatenate([jnp.concatenate([k[0], k[1]], axis=1) for k in order], axis=0)
            low = jnp.concatenate([jnp.concatenate([k[1], k[2]], axis=1) for k in order], axis=0)
            mixed[slot, g] = dot(left[part, g], jnp.concatenate([top, low], axis=0))

    def copies(step):
        slot = step % SLOTS
        chunk = chunk_of(lax.shift_right_logical(step, 2))
        for o in range(2):
            lanes = pl.ds(pl.multiple_of((chunk + 4 * o) * FACTOR, FACTOR), FACTOR)
            yield pltpu.make_async_copy(
                stage.at[slot, o], out.at[pl.ds((step & 3) * M_STEP, M_STEP), :, lanes], done.at[slot, o]
            )

    def spread(slot, step):
        target = step % SLOTS
        for t in range(8):
            for o in range(2):
                halves = []
                for h in range(2):
                    lanes = slice(o * FACTOR, (o + 1) * FACTOR)
                    parts = [mixed[slot, g, 16 * t + 8 * h : 16 * t + 8 * h + 8, lanes] for g in range(GROUPS)]
                    halves.append(spiral(parts, bits))
                for m in range(M_STEP):
                    pair = [pltpu.roll(x[-m % GROUPS], FACTOR - WIDTH * m, 1) if m else x[0] for x in halves]
                    stage[target, o, m, 16 * t : 16 * t + 16, :] = jnp.concatenate(pair, axis=0).astype(BF16)

    steps = count * (COUNT // M_STEP)
    prepare(jnp.int32(0), 0)
    prepare(jnp.int32(1), 1)
    multiply(jnp.int32(0), 0)

    def both(i, carry):
        for slot in range(2):
            step = 2 * i + slot

            @pl.when(step >= SLOTS)
            def _():
                for copy in copies(step - SLOTS):
                    copy.wait()

            prepare(jnp.minimum(step + 2, steps - 1), slot)
            multiply(jnp.minimum(step + 1, steps - 1), 1 - slot)
            spread(slot, step)
            for copy in copies(step):
                copy.start()
        return carry

    lax.fori_loop(0, steps // 2, both, 0)
    for step in range(steps - SLOTS, steps):
        for copy in copies(jnp.int32(step)):
            copy.wait()


def cross(parts, mine, theirs, rows, before):
    args = [*mine, *theirs, rows]
    specs = [VMEM] * len(args)
    aliases = {}
    if before is not None:
        aliases = {len(args): 0}
        args.append(before)
        specs.append(pl.BlockSpec(memory_space=pl.ANY))
    return pl.pallas_call(
        functools.partial(cross_kernel, parts),
        in_specs=specs,
        out_specs=pl.BlockSpec(memory_space=pl.ANY),
        scratch_shapes=[
            pltpu.VMEM((len(parts), GROUPS, FACTOR, 2 * FACTOR), BF16),
            pltpu.VMEM((2, WINDOWS, 3, 8, FACTOR), F32),
            pltpu.VMEM((2, GROUPS, FACTOR, 2 * FACTOR), F32),
            pltpu.VMEM((SLOTS, 2, M_STEP, FACTOR, FACTOR), BF16),
            pltpu.SemaphoreType.DMA((SLOTS, 2)),
        ],
        out_shape=jax.ShapeDtypeStruct((COUNT, 128, 2 * BAND), BF16),
        input_output_aliases=aliases,
        compiler_params=pltpu.CompilerParams(vmem_limit_bytes=LIMIT),
    )(*args)


CHAN = ("z", "x", "c")
WIN = ("y", "h")


def shards(samples, fir_taps, tap_counts, band_start, grid_blocks):
    tail = lax.ppermute(samples[:, -FACTOR:], WIN, [(i, i + 1) for i in range(WINDOWS - 1)])
    settings = jnp.concatenate(
        [fir_taps, tap_counts.astype(F32), band_start.astype(F32), jnp.zeros((FACTOR - 2,), F32)]
    )
    pieces = pl.pallas_call(
        front_kernel,
        in_specs=[VMEM, VMEM, VMEM, VMEM],
        out_specs=VMEM,
        out_shape=jax.ShapeDtypeStruct((COUNT, 8, FACTOR), BF16),
        scratch_shapes=[pltpu.VMEM((16, COUNT, FACTOR), F32), pltpu.VMEM((COUNT, FACTOR), F32)],
        compiler_params=pltpu.CompilerParams(vmem_limit_bytes=LIMIT),
    )(
        settings.reshape(1, 2 * FACTOR),
        samples.reshape(COUNT, FACTOR, FACTOR),
        tail,
        tables(),
    )
    every = lax.all_to_all(pieces, CHAN, 0, 0, tiled=True)
    sent = pl.pallas_call(
        pack_kernel,
        in_specs=[SMEM, VMEM],
        out_specs=VMEM,
        out_shape=jax.ShapeDtypeStruct((COUNT, 12, 8, FACTOR), BF16),
        compiler_params=SMALL,
    )(grid_blocks, every)
    got = lax.all_to_all(sent, ("z", *WIN), 0, 0, tiled=True)
    cols = got[:, :4]
    rows = pl.pallas_call(
        turn_kernel,
        in_specs=[VMEM],
        out_specs=VMEM,
        out_shape=jax.ShapeDtypeStruct((8, COUNT, 8, FACTOR), BF16),
        compiler_params=SMALL,
    )(got)
    last, rows = lax.optimization_barrier((cols, rows))
    mine = [cols] + [
        lax.ppermute(last if d == 2 else cols, "x", [(i, i ^ d) for i in range(4)]) for d in (1, 2, 3)
    ]
    theirs = [lax.ppermute(this, "c", [(0, 1), (1, 0)]) for this in mine]
    rows = lax.all_to_all(rows, ("x", "c"), 0, 0, tiled=True)
    return cross((0, 1, 2, 3), mine, theirs, rows, None)


def solution(mesh):
    fine = jax.sharding.Mesh(mesh.devices.reshape(4, 4, 2, 4, 2), (*CHAN, *WIN))
    placed = (P(CHAN, WIN), P(), P(WIN), P(), P())
    return jax.shard_map(
        shards, mesh=fine, in_specs=placed, out_specs=P(CHAN, WIN, None), check_vma=False
    )
```

```python
import functools
import math

import jax
import jax.numpy as jnp
import numpy as np
from jax import lax
from jax.experimental import pallas as pl
from jax.experimental.pallas import tpu as pltpu
from jax.sharding import PartitionSpec as P

LEN = 16384
FACTOR = 128
BAND = 512
KMAX = 128
COUNT = 32
QUARTERS = BAND // FACTOR
WINDOWS = 8
BATCH = 16
GROUPS = 8
WIDTH = FACTOR // GROUPS
SLOTS = 4
LIMIT = 48 * 1024 * 1024
SMALL = pltpu.CompilerParams(vmem_limit_bytes=8 * 1024 * 1024)

VMEM = pl.BlockSpec(memory_space=pltpu.VMEM)
SMEM = pl.BlockSpec(memory_space=pltpu.SMEM)
BF16 = jnp.bfloat16
F32 = jnp.float32


def tables():
    index = np.arange(FACTOR)
    angles = np.mod(index[:, None] * index[None, :], FACTOR) * (2.0 * math.pi / FACTOR)
    theta = index[:, None] * index[None, :] * (2.0 * math.pi / LEN)
    parts = [np.cos(angles), -np.sin(angles), np.cos(theta), -np.sin(theta)]
    return np.concatenate(parts).astype(np.float32)


def dot(a, b):
    return jnp.dot(a, b, preferred_element_type=F32)


def dot_t(a, b):
    return lax.dot_general(a, b, (((1,), (1,)), ((), ())), preferred_element_type=F32)


def front_kernel(settings, x, tail, table, out, product, before):
    window = lax.axis_index("y") * 2 + lax.axis_index("h")
    lane = lax.broadcasted_iota(jnp.int32, (1, FACTOR), 1)
    used = jnp.broadcast_to(settings[:, FACTOR : FACTOR + 1], (1, FACTOR)).astype(jnp.int32)
    start = jnp.broadcast_to(settings[:, FACTOR + 1 : FACTOR + 2], (1, FACTOR)).astype(jnp.int32)
    kept = jnp.where(lane < used, settings[:, :FACTOR], 0.0)
    kept = jnp.concatenate([kept, jnp.zeros_like(kept)], axis=1)
    spread = jnp.broadcast_to(kept, (2 * FACTOR, 2 * FACTOR))
    matrix = pltpu.roll(spread, FACTOR, 1, stride=1, stride_axis=0)[:, :FACTOR].astype(BF16)
    both = jnp.concatenate([matrix[FACTOR:], matrix[:FACTOR]], axis=1)
    before[...] = dot(tail[...], matrix[:FACTOR])
    first = table[: 2 * FACTOR].astype(BF16)
    low = lax.shift_right_logical(start, 7)
    row = lax.broadcasted_iota(jnp.int32, (8, FACTOR), 0)
    pick = (lax.broadcasted_iota(jnp.int32, (8, FACTOR), 1) == low + row).astype(F32).astype(BF16)
    cosine = dot(pick, first[:FACTOR])
    sine = dot(pick, first[FACTOR:])
    second = jnp.concatenate(
        [jnp.concatenate([cosine, -sine], axis=1), jnp.concatenate([sine, cosine], axis=1)], axis=0
    )
    second = (second * (1.0 / FACTOR)).astype(BF16)
    top = lax.broadcasted_iota(jnp.int32, (FACTOR, FACTOR), 0) == 0

    def some(i, carry):
        y = dot(x[pl.ds(BATCH * i, BATCH)].reshape(BATCH * FACTOR, FACTOR), both)
        parts = []
        for j in range(BATCH):
            now = y[j * FACTOR : (j + 1) * FACTOR]
            late = jnp.where(top, before[pl.ds(BATCH * i + j, 1), :], pltpu.roll(now[:, FACTOR:], 1, 0))
            parts.append((now[:, :FACTOR] + late).astype(BF16))
        section = dot(first, jnp.concatenate(parts, axis=1))
        halves = []
        for j in range(BATCH):
            re = section[:FACTOR, j * FACTOR : (j + 1) * FACTOR]
            im = section[FACTOR:, j * FACTOR : (j + 1) * FACTOR]
            twist_re = table[2 * FACTOR : 3 * FACTOR]
            twist_im = table[3 * FACTOR :]
            halves.append(
                jnp.concatenate([re * twist_re - im * twist_im, re * twist_im + im * twist_re], axis=1).astype(BF16)
            )
        got = dot_t(second, jnp.concatenate(halves, axis=0))
        for j in range(BATCH):
            product[:, pl.ds(BATCH * i + j, 1), :] = got[:, None, j * FACTOR : (j + 1) * FACTOR]
        return carry

    lax.fori_loop(0, COUNT // BATCH, some, 0)

    early = lax.broadcasted_iota(jnp.int32, (COUNT, FACTOR), 1) >= (start & (FACTOR - 1))
    residue = lax.broadcasted_iota(jnp.int32, (FACTOR, BAND), 0)
    lane = lax.broadcasted_iota(jnp.int32, (FACTOR, BAND), 1)
    place = (lane & -FACTOR) + ((lane - WIDTH * window) & (FACTOR - 1))
    placed = None
    for q in range(QUARTERS):
        re = jnp.where(early, product[q], product[q + 1])
        im = jnp.where(early, product[8 + q], product[9 + q])
        scale = lax.rsqrt(re * re + im * im + 1.0)
        white = jnp.concatenate([re * scale, im * scale], axis=0).astype(BF16)
        moved = dot(white, (place == QUARTERS * residue + q).astype(F32).astype(BF16))
        placed = moved if placed is None else placed + moved
    for z in range(4):
        for quarter in range(4):
            for o in range(2):
                at = o * COUNT + z * 8
                piece = placed[at : at + 8, quarter * FACTOR : (quarter + 1) * FACTOR]
                out[z * 8 + quarter * 2 + o] = piece.astype(BF16)


def pack_kernel(blocks, every, out):
    for i in range(COUNT):
        block = every[blocks[i]]
        for z in range(4):
            out[z * WINDOWS + i // 4, i % 4] = block
        for j in range(WINDOWS):
            out[i // 8 * WINDOWS + j, 4 + i % 8] = block


def turn_kernel(got, out):
    for i in range(COUNT):
        for r in range(8):
            out[r, i] = got[i, 4 + r]


M_STEP = 8


def spiral(parts, bits):
    for s in range(3):
        parts = [jnp.where(bits[s], parts[(a + (1 << s)) % GROUPS], parts[a]) for a in range(GROUPS)]
    return parts


def cross_kernel(parts, *refs):
    count = len(parts)
    mine, theirs, rows = refs[:count], refs[count : 2 * count], refs[2 * count]
    out, left, coef, mixed, stage, done = refs[-6:]
    x, core = lax.axis_index("x"), lax.axis_index("c")
    spot = lax.broadcasted_iota(jnp.int32, (8, FACTOR), 1) // WIDTH
    bits = [(spot & (1 << s)) != 0 for s in range(3)]
    inner = lax.broadcasted_iota(jnp.int32, (WIDTH, FACTOR), 0)
    lane = lax.broadcasted_iota(jnp.int32, (WIDTH, FACTOR), 1)
    diagonal = inner == (lane & (WIDTH - 1))

    def cols(part, b, carry):
        for pair in range(2):
            tiles = []
            for half in range(2):
                d = 2 * pair + half
                whole = [[], []]
                for w in range(WINDOWS):
                    a = mine[part][d * WINDOWS + w, b].astype(F32)
                    t = theirs[part][d * WINDOWS + w, b].astype(F32)
                    whole[0].append(jnp.where(core == 0, a, t))
                    whole[1].append(jnp.where(core == 0, t, a))
                tiles.append([spiral(whole[i], bits) for i in range(2)])
            at = pl.multiple_of(b * 32 + pair * 16, 16)
            for g in range(GROUPS):
                for i in range(2):
                    packed = jnp.concatenate([tiles[h][i][-g % GROUPS] for h in range(2)], axis=0)
                    left[part, g, pl.ds(at, 16), i * FACTOR : (i + 1) * FACTOR] = packed.astype(BF16)
        return carry

    for part in range(count):
        lax.fori_loop(0, 4, functools.partial(cols, part), 0)

    def chunk_of(part):
        turn = jnp.int32(parts[0])
        for i in range(1, count):
            turn = jnp.where(part == i, parts[i], turn)
        return x ^ turn

    def prepare(step, slot):
        part = lax.shift_right_logical(step, 2)
        at = chunk_of(part) * 2
        z = step & 3
        for w in range(WINDOWS):
            for i in range(2):
                u = rows[at + i, z * WINDOWS + w].astype(F32)
                if w:
                    u = pltpu.roll(u, FACTOR - WIDTH * w, 1)
                u = pltpu.roll(u, 0, 1, stride=WIDTH, stride_axis=0)
                for s in range(3):
                    u = jnp.where(bits[s], pltpu.roll(u, 8 - (1 << s), 0), u)
                coef[slot, w, i] = u
                if i == 0:
                    coef[slot, w, 2] = -u

    def multiply(step, slot):
        part = lax.shift_right_logical(step, 2)
        for g in range(GROUPS):
            blocks = [
                [
                    jnp.where(diagonal, coef[slot, w, i, pl.ds(-g % GROUPS, 1), :], 0.0).astype(BF16)
                    for i in range(3)
                ]
                for w in range(WINDOWS)
            ]
            order = [blocks[(c - g) % GROUPS] for c in range(GROUPS)]
            top = jnp.concatenate([jnp.concatenate([k[0], k[1]], axis=1) for k in order], axis=0)
            low = jnp.concatenate([jnp.concatenate([k[1], k[2]], axis=1) for k in order], axis=0)
            mixed[slot, g] = dot(left[part, g], jnp.concatenate([top, low], axis=0))

    def copies(step):
        slot = step % SLOTS
        chunk = chunk_of(lax.shift_right_logical(step, 2))
        for o in range(2):
            lanes = pl.ds(pl.multiple_of((chunk + 4 * o) * FACTOR, FACTOR), FACTOR)
            yield pltpu.make_async_copy(
                stage.at[slot, o], out.at[pl.ds((step & 3) * M_STEP, M_STEP), :, lanes], done.at[slot, o]
            )

    def spread(slot, step):
        target = step % SLOTS
        for t in range(8):
            for o in range(2):
                halves = []
                for h in range(2):
                    lanes = slice(o * FACTOR, (o + 1) * FACTOR)
                    parts = [mixed[slot, g, 16 * t + 8 * h : 16 * t + 8 * h + 8, lanes] for g in range(GROUPS)]
                    halves.append(spiral(parts, bits))
                for m in range(M_STEP):
                    pair = [pltpu.roll(x[-m % GROUPS], FACTOR - WIDTH * m, 1) if m else x[0] for x in halves]
                    stage[target, o, m, 16 * t : 16 * t + 16, :] = jnp.concatenate(pair, axis=0).astype(BF16)

    steps = count * (COUNT // M_STEP)
    prepare(jnp.int32(0), 0)
    prepare(jnp.int32(1), 1)
    multiply(jnp.int32(0), 0)

    def both(i, carry):
        for slot in range(2):
            step = 2 * i + slot

            @pl.when(step >= SLOTS)
            def _():
                for copy in copies(step - SLOTS):
                    copy.wait()

            prepare(jnp.minimum(step + 2, steps - 1), slot)
            multiply(jnp.minimum(step + 1, steps - 1), 1 - slot)
            spread(slot, step)
            for copy in copies(step):
                copy.start()
        return carry

    lax.fori_loop(0, steps // 2, both, 0)
    for step in range(steps - SLOTS, steps):
        for copy in copies(jnp.int32(step)):
            copy.wait()


def cross(parts, mine, theirs, rows, before):
    args = [*mine, *theirs, rows]
    specs = [VMEM] * len(args)
    aliases = {}
    if before is not None:
        aliases = {len(args): 0}
        args.append(before)
        specs.append(pl.BlockSpec(memory_space=pl.ANY))
    return pl.pallas_call(
        functools.partial(cross_kernel, parts),
        in_specs=specs,
        out_specs=pl.BlockSpec(memory_space=pl.ANY),
        scratch_shapes=[
            pltpu.VMEM((len(parts), GROUPS, FACTOR, 2 * FACTOR), BF16),
            pltpu.VMEM((2, WINDOWS, 3, 8, FACTOR), F32),
            pltpu.VMEM((2, GROUPS, FACTOR, 2 * FACTOR), F32),
            pltpu.VMEM((SLOTS, 2, M_STEP, FACTOR, FACTOR), BF16),
            pltpu.SemaphoreType.DMA((SLOTS, 2)),
        ],
        out_shape=jax.ShapeDtypeStruct((COUNT, 128, 2 * BAND), BF16),
        input_output_aliases=aliases,
        compiler_params=pltpu.CompilerParams(vmem_limit_bytes=LIMIT),
    )(*args)


CHAN = ("z", "x", "c")
WIN = ("y", "h")


def shards(samples, fir_taps, tap_counts, band_start, grid_blocks):
    tail = lax.ppermute(samples[:, -FACTOR:], WIN, [(i, i + 1) for i in range(WINDOWS - 1)])
    settings = jnp.concatenate(
        [fir_taps, tap_counts.astype(F32), band_start.astype(F32), jnp.zeros((FACTOR - 2,), F32)]
    )
    pieces = pl.pallas_call(
        front_kernel,
        in_specs=[VMEM, VMEM, VMEM, VMEM],
        out_specs=VMEM,
        out_shape=jax.ShapeDtypeStruct((COUNT, 8, FACTOR), BF16),
        scratch_shapes=[pltpu.VMEM((16, COUNT, FACTOR), F32), pltpu.VMEM((COUNT, FACTOR), F32)],
        compiler_params=pltpu.CompilerParams(vmem_limit_bytes=LIMIT),
    )(
        settings.reshape(1, 2 * FACTOR),
        samples.reshape(COUNT, FACTOR, FACTOR),
        tail,
        tables(),
    )
    every = lax.all_to_all(pieces, CHAN, 0, 0, tiled=True)
    sent = pl.pallas_call(
        pack_kernel,
        in_specs=[SMEM, VMEM],
        out_specs=VMEM,
        out_shape=jax.ShapeDtypeStruct((COUNT, 12, 8, FACTOR), BF16),
        compiler_params=SMALL,
    )(grid_blocks, every)
    got = lax.all_to_all(sent, ("z", *WIN), 0, 0, tiled=True)
    cols = got[:, :4]
    rows = pl.pallas_call(
        turn_kernel,
        in_specs=[VMEM],
        out_specs=VMEM,
        out_shape=jax.ShapeDtypeStruct((8, COUNT, 8, FACTOR), BF16),
        compiler_params=SMALL,
    )(got)
    last, rows = lax.optimization_barrier((cols, rows))
    mine = [cols] + [
        lax.ppermute(last if d == 2 else cols, "x", [(i, i ^ d) for i in range(4)]) for d in (1, 2, 3)
    ]
    theirs = [lax.ppermute(this, "c", [(0, 1), (1, 0)]) for this in mine]
    rows = lax.all_to_all(rows, ("x", "c"), 0, 0, tiled=True)
    return cross((0, 1, 2, 3), mine, theirs, rows, None)


def solution(mesh):
    fine = jax.sharding.Mesh(mesh.devices.reshape(4, 4, 2, 4, 2), (*CHAN, *WIN))
    placed = (P(CHAN, WIN), P(), P(WIN), P(), P())
    return jax.shard_map(
        shards, mesh=fine, in_specs=placed, out_specs=P(CHAN, WIN, None), check_vma=False
    )
```
